32 devices in a mesh: tm: 32 (over z, y, x, core), sta: 1.
Axes of the slice: x: 2, y: 2, z: 4, core: 2. Of those that a mesh axis runs over, the one named last changes fastest.
Arguments:
- record: float32 [192, 16384], P('sta', 'tm'), may hold values from -200 to 200
- owner: int32 [96, 1], replicated, may hold values from 0 to 31; in each aligned block of 32 rows (0 to 31, 32 to 63, ...) at most 2 rows name the same one
- offset: int32 [96], replicated, may hold values from 0 to 511
- station: int32 [192], P('sta'), may hold values from 0 to 63, as said below
- valid: int32 [192], P('sta'), may hold values 0 or 1
Outputs:
- stack: float32 [3, 32, 16384], P(None, 'sta', 'tm')
The draws below stay inside these ranges and needn't reach their ends.
Inputs may be any that keep to these rules, and one draw needn't show every extreme that they name: `owner`: among the 32 templates of one step (rows i * 32 to i * 32 + 31) no time block is named more than 2 times, and some block is named exactly 2 times in some step. Every station number names exactly 3 channels.
All inputs are finite; a program needn't handle non-finite values. No bound on the sum of `valid` on one device may be relied on, other than what follows from the above.
Results may differ from the reference program's by a relative error of at most 0.0015.
Values may be sent and summed in bfloat16 or wider, within the bound.
A program may use at most 64 MiB of HBM per device.

```python
import math
import jax
import jax.numpy as jnp
import numpy as np
from jax import lax

WIN = 100
S_DEV = 512
TPL_STEP = 32
NSTEP = 3
NTPL = 96
CHANNELS = 192
SAMPLES = 16384
NSTATIONS = 64
MOST = 2
N_TM = 32


def draw_record(key, part):
    noise_key, gain_key, envelope_key = jax.random.split(key, 3)
    noise = jnp.clip(jax.random.normal(noise_key, (CHANNELS, SAMPLES), jnp.float32), -6.0, 6.0)
    gains = jnp.exp(jax.random.uniform(gain_key, (CHANNELS, 1), jnp.float32, 0.0, math.log(10.0)))
    envelope = jnp.exp(jax.random.uniform(envelope_key, (CHANNELS, SAMPLES // 32, 1), jnp.float32, -1.0, 1.0))
    envelope = jnp.broadcast_to(envelope, (CHANNELS, SAMPLES // 32, 32)).reshape(CHANNELS, SAMPLES)
    return (noise * gains * envelope).astype(jnp.float32)


def draw_station(key, part):
    shuffled = jax.random.permutation(key, CHANNELS)
    return (shuffled // 3).astype(jnp.int32)


def place_ends(entries, own_key, least, high):
    index_at = [jax.random.randint(jax.random.fold_in(own_key, axis), (), 0, length) for axis, length in enumerate(entries.shape)]
    main_axis = entries.shape.index(max(entries.shape))
    beside = index_at[:main_axis] + [(index_at[main_axis] + 1) % entries.shape[main_axis]] + index_at[main_axis + 1:]
    return entries.at[tuple(index_at)].set(least).at[tuple(beside)].set(high)


def routed_block(rng, own, number, rows, amount, top, bound, skew):
    order = jax.random.permutation(rng, amount)
    packed, ordinary = shares(amount, rows * top, bound, skew, True), shares(amount, rows * top, bound, skew, False)
    places = jnp.arange(amount)

    def named(sizes, turn):
        used = int((sizes > 0).sum())
        fixed = max(1, used // 4)
        moved = fixed + (places - fixed + turn * (used - fixed)) % max(1, amount - fixed)
        return jnp.zeros((amount,), jnp.int32).at[order[jnp.where(places < fixed, places, moved)]].set(jnp.asarray(sizes, jnp.int32))

    sizes = jnp.where(number % 4 == 0, named(packed, number // 4), named(ordinary, number - number // 4 - 1))
    mixed = jax.random.permutation(jax.random.fold_in(own, 3), amount)
    source_of, sink = mixed[0:amount // 2 * 2:2], mixed[1:amount // 2 * 2:2]
    margin = jnp.minimum(sizes[source_of] - 1, bound - sizes[sink]) // 2
    margin = jnp.where((source_of == order[0]) | (sink == order[0]) | (sizes[sink] == 0), 0, jnp.maximum(margin, 0))
    moved = jax.random.randint(jax.random.fold_in(own, 4), (amount // 2,), 0, 1 << 20) % (margin + 1)
    sizes = sizes.at[source_of].add(-moved).at[sink].add(moved)
    labels = jnp.searchsorted(jnp.cumsum(sizes), jnp.arange(rows * top), side="right").astype(jnp.int32)
    table = labels.reshape(top, rows).T
    table = table[jax.random.permutation(jax.random.fold_in(own, 1), rows)]
    turn = jax.random.randint(jax.random.fold_in(own, 2), (rows, 1), 0, top)
    return jnp.take_along_axis(table, (jnp.arange(top)[None, :] + turn) % top, axis=1)


def shares(number_of, total, most, skew, full):
    portions = [(1 << 20) // math.isqrt(standing ** skew) + 1 for standing in range(1, number_of + 1)]
    largest = most if full else min(most, max(-(-total // number_of), total * portions[0] // sum(portions)))
    least = 1 if total - largest >= number_of - 1 else 0
    given, rest = [largest] + [least] * (number_of - 1), total - largest - least * (number_of - 1)
    while rest > 0:
        candidates = [i for i in range(1, number_of) if given[i] < largest] or [i for i in range(1, number_of) if given[i] < most]
        pool, left = sum([portions[i] for i in candidates]), rest
        for i in candidates:
            more = min(most - given[i], max(1, left * portions[i] // pool), rest)
            given[i] = given[i] + more
            rest = rest - more
    return np.array(given)


def setup_inputs(seed: int = 0) -> dict:
    splits = jax.random.split(jax.random.key(seed), 6)
    record = draw_record(jax.random.fold_in(splits[5], 71), 0)
    owner_keys = jax.random.split(jax.random.fold_in(splits[1], 1), NTPL // TPL_STEP)
    owner_turns = jax.random.permutation(jax.random.fold_in(splits[1], 3), NTPL // TPL_STEP)
    owner = jax.vmap(lambda own, number: routed_block(jax.random.fold_in(splits[1], 2), own, number, TPL_STEP, N_TM, 1, MOST, 2))(owner_keys, owner_turns).reshape((NTPL, 1))
    offset = place_ends(jax.random.randint(splits[2], (NTPL,), 0, S_DEV), jax.random.fold_in(splits[2], 1), 0, S_DEV - 1).astype(jnp.int32)
    station = draw_station(jax.random.fold_in(splits[5], 71), 0)
    valid = place_ends((jax.random.randint(splits[4], (CHANNELS,), 0, 5) < 4).astype(jnp.int32), jax.random.fold_in(splits[4], 1), 0, 1)
    return {"record": record, "owner": owner, "offset": offset, "station": station, "valid": valid}


EPSILON = 1e-05

def normalize(pieces):
    values = pieces.astype(jnp.float32)
    centred = values - lax.optimization_barrier(jnp.mean(values, axis=-1, keepdims=True))
    spread = jnp.sqrt(lax.optimization_barrier(jnp.mean(centred * centred, axis=-1, keepdims=True)) + EPSILON)
    return (centred / (WIN * spread)).astype(jnp.bfloat16)

def reference(record, owner, offset, station, valid):
    extended = jnp.concatenate([record.astype(jnp.bfloat16), jnp.zeros((CHANNELS, WIN - 1), jnp.bfloat16)], axis=1)
    starts = owner[:, 0].astype(jnp.int32) * SAMP_FACTOR_FIX(S_DEV) + offset.astype(jnp.int32)

    def template_at(first_sample):
        return lax.dynamic_slice_in_dim(extended, first_sample, WIN, 1)
    templates = normalize(lax.map(template_at, starts))
    present = valid.astype(jnp.float32)
    counts = jax.ops.segment_sum(present, station.astype(jnp.int32), num_segments=NSTATIONS)
    weight = present / jnp.maximum(counts[station.astype(jnp.int32)], 1.0)
    block_size = 8
    block_count = CHANNELS // block_size

    def add_block(running, block_index):
        channel_rows = lax.dynamic_slice_in_dim(extended, block_index * block_size, block_size, 0)
        hankel = jnp.stack([channel_rows[:, k:k + SAMPLES] for k in range(WIN)], axis=1)
        values = hankel.astype(jnp.float32)
        window_mean = lax.optimization_barrier(jnp.mean(values, axis=1))
        window_square = lax.optimization_barrier(jnp.mean(values * values, axis=1))
        inverse = 1.0 / jnp.sqrt(jnp.maximum(window_square - window_mean * window_mean, 0.0) + EPSILON)
        scaled = lax.dynamic_slice_in_dim(weight, block_index * block_size, block_size, 0)
        window = (values * (scaled[:, None] * inverse)[:, None, :]).astype(jnp.bfloat16)
        template_part = lax.dynamic_slice_in_dim(templates, block_index * block_size, block_size, 1)
        template_part = template_part.reshape(NTPL, block_size * WIN)
        product = jnp.dot(template_part, window.reshape(block_size * WIN, SAMPLES), preferred_element_type=jnp.float32)
        return (running + product, None)
    running, unused = lax.scan(add_block, jnp.zeros((NTPL, SAMPLES), jnp.float32), jnp.arange(block_count, dtype=jnp.int32))
    result = running / math.sqrt(NSTATIONS)
    return result.reshape(NSTEP, TPL_STEP, SAMPLES)

def SAMP_FACTOR_FIX(value):
    return value
```

```python
import functools
import math

import jax
import jax.numpy as jnp
from jax import lax
from jax.experimental import pallas as pl
from jax.experimental.pallas import tpu as pltpu
from jax.sharding import PartitionSpec as P

WIN = 100
TPL_STEP = 32
NSTEP = 3
EPSILON = 1e-05
GROUP = 8
SHIFTS = 5
LANES = 128
TAIL = 128
MESH = pl.DeviceIdType.MESH
VMEM = pl.BlockSpec(memory_space=pltpu.VMEM)
SMEM = pl.BlockSpec(memory_space=pltpu.SMEM)


def exchange_kernel(n, mine_ref, all_ref, send_sem, recv_sem, own_sem):
    me = lax.axis_index("tm")
    barrier = pltpu.get_barrier_semaphore()

    def greet(d, carry):
        pl.semaphore_signal(
            barrier, inc=1, device_id={"tm": lax.rem(me + d, n)}, device_id_type=MESH
        )
        return carry

    lax.fori_loop(1, n, greet, 0)
    own = pltpu.make_async_copy(mine_ref.at[lax.rem(me, GROUP)], all_ref.at[me], own_sem)
    own.start()
    pl.semaphore_wait(barrier, n - 1)

    def send(d, carry):
        to = lax.rem(me + d, n)
        pltpu.make_async_remote_copy(
            src_ref=mine_ref.at[lax.rem(to, GROUP)],
            dst_ref=all_ref.at[me],
            send_sem=send_sem.at[d],
            recv_sem=recv_sem.at[me],
            device_id={"tm": to},
            device_id_type=MESH,
        ).start()
        return carry

    lax.fori_loop(1, n, send, 0)

    def finish(d, carry):
        source = lax.rem(me + n - d, n)
        copy = pltpu.make_async_remote_copy(
            src_ref=mine_ref.at[0],
            dst_ref=all_ref.at[source],
            send_sem=send_sem.at[d],
            recv_sem=recv_sem.at[source],
            device_id={"tm": source},
            device_id_type=MESH,
        )
        copy.wait_send()
        copy.wait_recv()
        return carry

    lax.fori_loop(1, n, finish, 0)
    own.wait()


def exchange(mine, n):
    return pl.pallas_call(
        functools.partial(exchange_kernel, n),
        out_shape=jax.ShapeDtypeStruct((n,) + mine.shape[1:], mine.dtype),
        in_specs=[VMEM],
        out_specs=VMEM,
        scratch_shapes=[
            pltpu.SemaphoreType.DMA((n,)),
            pltpu.SemaphoreType.DMA((n,)),
            pltpu.SemaphoreType.DMA,
        ],
        compiler_params=pltpu.CompilerParams(
            collective_id=0, has_side_effects=True, vmem_limit_bytes=32 * 1024 * 1024
        ),
    )(mine)


def ahead(array, by):
    return pltpu.roll(array, array.shape[1] - by, 1) if by else array


def window_sum(x):
    two = x + ahead(x, 1)
    four = two + ahead(two, 2)
    eight = four + ahead(four, 4)
    sixteen = eight + ahead(eight, 8)
    half = sixteen + ahead(sixteen, 16)
    full = half + ahead(half, 32)
    return full + ahead(half, 64) + ahead(four, 96)


def correlate_kernel(
    n, samp, factor, plane_ref, start_ref, all_ref, weight_ref, out_ref,
    chan, rows, raw, tpl, gain, win,
):
    parts = all_ref.shape[1] // 2
    half = samp // 2
    rows_in = SHIFTS * parts
    steps = WIN // SHIFTS
    count = start_ref.shape[0]
    total = n * samp

    def spread(j, carry):
        block = all_ref[j].astype(jnp.float32)
        chan[:, pl.ds(pl.multiple_of(j * samp, samp), half)] = block[:parts]
        chan[:, pl.ds(pl.multiple_of(j * samp + half, half), half)] = block[parts:]
        return carry

    lax.fori_loop(0, n, spread, 0)
    chan[:, pl.ds(total, TAIL)] = jnp.zeros((parts, TAIL), jnp.float32)

    def turn(b, carry):
        at = pl.multiple_of(b * samp, samp)
        values = chan[:, pl.ds(at, samp + TAIL)]
        pieces = [ahead(values, k)[:, :samp] for k in range(SHIFTS)]
        pieces.append(jnp.zeros((LANES - rows_in, samp), jnp.float32))
        rows[pl.ds(at, samp), :] = jnp.concatenate(pieces, axis=0).T
        return carry

    lax.fori_loop(0, n, turn, 0)
    rows[pl.ds(total, TAIL), :] = jnp.zeros((TAIL, LANES), jnp.float32)

    def pick(t, carry):
        raw[pl.ds(t, 24, stride=count), :] = rows[pl.ds(start_ref[t], 24, stride=SHIFTS), :]
        return carry

    lax.fori_loop(0, count, pick, 0)
    lane_a = lax.broadcasted_iota(jnp.int32, (LANES, LANES), 0)
    lane_b = lax.broadcasted_iota(jnp.int32, (LANES, LANES), 1)
    same = (lax.rem(lane_a, parts) == lax.rem(lane_b, parts)) & (
        (lane_a < rows_in) & (lane_b < rows_in)
    )
    fold = jnp.where(same, 1.0, 0.0).astype(jnp.float32)

    def folded(x):
        return jnp.dot(
            x, fold, precision=lax.Precision.HIGHEST, preferred_element_type=jnp.float32
        )

    sums = raw[pl.ds(0, count), :]
    for j in range(1, steps):
        sums = sums + raw[pl.ds(j * count, count), :]
    mean = folded(sums) / WIN
    square = jnp.zeros_like(mean)
    for j in range(steps):
        centred = raw[pl.ds(j * count, count), :] - mean
        square = square + centred * centred
    spread_of = jnp.sqrt(folded(square) / WIN + EPSILON)
    scale = 1.0 / (WIN * spread_of)
    for j in range(steps):
        value = (raw[pl.ds(j * count, count), :] - mean) * scale
        tpl[pl.ds(0, count), pl.ds(j * LANES, LANES)] = value.astype(jnp.bfloat16)
    tpl[pl.ds(count, LANES - count), :] = jnp.zeros(
        (LANES - count, tpl.shape[1]), jnp.bfloat16
    )
    weight = weight_ref[...]
    first = plane_ref[0] * (GROUP * samp)
    sub = 64

    def stack(i, carry):
        base = pl.multiple_of(first + i * samp, samp)
        values = chan[:, pl.ds(base, samp + TAIL)]
        a = window_sum(values)[:, :samp] / WIN
        q = window_sum(values * values)[:, :samp] / WIN
        inverse = 1.0 / jnp.sqrt(jnp.maximum(q - a * a, 0.0) + EPSILON)
        g = weight * inverse
        gain[...] = jnp.concatenate(
            [g] * SHIFTS + [jnp.zeros((LANES - rows_in, samp), jnp.float32)], axis=0
        ).T

        def fill(r, inner):
            at = pl.multiple_of(r * sub, sub)
            scaled = gain[pl.ds(at, sub), :]
            for j in range(steps):
                x = rows[pl.ds(base + at + j * SHIFTS, sub), :]
                win[pl.ds(at, sub), pl.ds(j * LANES, LANES)] = (x * scaled).astype(jnp.bfloat16)
            return inner

        lax.fori_loop(0, samp // sub, fill, 0)
        product = lax.dot_general(
            win[...], tpl[...], (((1,), (1,)), ((), ())), preferred_element_type=jnp.float32
        )
        slot = lax.rem(i, 2) * (GROUP // 2) + i // 2
        out_ref[slot] = product.T[:count] * factor
        return carry

    lax.fori_loop(0, GROUP, stack, 0)


def correlate(everyone, start, weight, plane, n, samp, factor):
    parts = everyone.shape[1] // 2
    count = start.shape[0]
    total = n * samp
    deep = WIN // SHIFTS * LANES
    return pl.pallas_call(
        functools.partial(correlate_kernel, n, samp, factor),
        out_shape=jax.ShapeDtypeStruct((GROUP, count, samp), jnp.float32),
        in_specs=[SMEM, SMEM, VMEM, VMEM],
        out_specs=VMEM,
        scratch_shapes=[
            pltpu.VMEM((parts, total + TAIL), jnp.float32),
            pltpu.VMEM((total + TAIL, LANES), jnp.float32),
            pltpu.VMEM((24 * count, LANES), jnp.float32),
            pltpu.VMEM((LANES, deep), jnp.bfloat16),
            pltpu.VMEM((samp, LANES), jnp.float32),
            pltpu.VMEM((samp, deep), jnp.bfloat16),
        ],
        compiler_params=pltpu.CompilerParams(vmem_limit_bytes=48 * 1024 * 1024),
    )(plane, start, everyone, weight)


def reduce_kernel(part_ref, out_ref, pair, far, mid, pair_send, pair_recv, far_send, far_recv):
    me = lax.axis_index("tm")
    chips = GROUP // 2
    base = (me // GROUP) * GROUP
    place = lax.rem(me, GROUP)
    core, chip = lax.rem(place, 2), place // 2
    other = base + chip * 2 + (1 - core)
    barrier = pltpu.get_barrier_semaphore()
    pl.semaphore_signal(barrier, inc=1, device_id={"tm": other}, device_id_type=MESH)
    for d in range(1, chips):
        to = base + lax.rem(chip + d, chips) * 2 + core
        pl.semaphore_signal(barrier, inc=1, device_id={"tm": to}, device_id_type=MESH)
    pl.semaphore_wait(barrier, chips)
    first = []
    for d in (2, 1, 3, 0):
        slot = lax.rem(chip + d, chips)
        copy = pltpu.make_async_remote_copy(
            src_ref=part_ref.at[1 - core, slot],
            dst_ref=pair.at[d],
            send_sem=pair_send.at[d],
            recv_sem=pair_recv.at[d],
            device_id={"tm": other},
            device_id_type=MESH,
        )
        copy.start()
        first.append((d, slot, copy))
    second = []
    for d, slot, copy in first:
        copy.wait_recv()
        if d:
            mid[d] = part_ref[core, slot] + pair[d]
            far_copy = pltpu.make_async_remote_copy(
                src_ref=mid.at[d],
                dst_ref=far.at[d],
                send_sem=far_send.at[d],
                recv_sem=far_recv.at[d],
                device_id={"tm": base + slot * 2 + core},
                device_id_type=MESH,
            )
            far_copy.start()
            second.append((d, far_copy))
        else:
            out_ref[...] = part_ref[core, slot] + pair[d]
    for d, far_copy in second:
        far_copy.wait_recv()
        out_ref[...] += far[d]
    for d, slot, copy in first:
        copy.wait_send()
    for d, far_copy in second:
        far_copy.wait_send()


def reduce_group(partial):
    chips = GROUP // 2
    shape = partial.shape[1:]
    block = pltpu.VMEM((chips,) + shape, jnp.float32)
    return pl.pallas_call(
        reduce_kernel,
        out_shape=jax.ShapeDtypeStruct(shape, jnp.float32),
        in_specs=[VMEM],
        out_specs=VMEM,
        scratch_shapes=[block, block, block]
        + [pltpu.SemaphoreType.DMA((chips,)) for unused in range(4)],
        compiler_params=pltpu.CompilerParams(
            collective_id=1, has_side_effects=True, vmem_limit_bytes=32 * 1024 * 1024
        ),
    )(partial.reshape((2, chips) + shape))


def body(record, owner, offset, station, valid):
    ch_dev, samp = record.shape
    n = lax.axis_size("tm")
    me = lax.axis_index("tm")
    parts = ch_dev // GROUP
    mine = record.astype(jnp.bfloat16).reshape(GROUP, parts, 2, samp // 2)
    mine = mine.transpose(0, 2, 1, 3).reshape(GROUP, 2 * parts, samp // 2)
    everyone = exchange(mine, n)

    stations = ch_dev * lax.axis_size("sta") // 3
    station_table = (station[:, None] == jnp.arange(stations, dtype=jnp.int32)[None, :]).astype(
        jnp.float32
    )
    present = valid.astype(jnp.float32)
    counts = lax.psum(jnp.sum(present[:, None] * station_table, axis=0), "sta")
    own_counts = jnp.sum(station_table * counts[None, :], axis=1)
    weight = present / jnp.maximum(own_counts, 1.0)
    own_weight = lax.dynamic_slice_in_dim(weight, lax.rem(me, GROUP) * parts, parts, 0)

    start = owner[:, 0] * samp + offset
    plane = (me // GROUP).reshape(1)
    factor = 1.0 / math.sqrt(stations)
    partial = correlate(everyone, start, own_weight[:, None], plane, n, samp, factor)
    stack = reduce_group(partial)
    stack = stack.reshape(NSTEP, TPL_STEP, samp)
    return lax.psum_scatter(stack, "sta", scatter_dimension=1, tiled=True)


def solution(mesh):
    placed = (P("sta", "tm"), P(), P(), P("sta"), P("sta"))
    return jax.shard_map(
        body, mesh=mesh, in_specs=placed, out_specs=P(None, "sta", "tm"), check_vma=False
    )
```

```python
import functools
import math

import jax
import jax.numpy as jnp
from jax import lax
from jax.experimental import pallas as pl
from jax.experimental.pallas import tpu as pltpu
from jax.sharding import PartitionSpec as P

WIN = 100
TPL_STEP = 32
NSTEP = 3
EPSILON = 1e-05
GROUP = 8
SHIFTS = 5
LANES = 128
TAIL = 256
MESH = pl.DeviceIdType.MESH
VMEM = pl.BlockSpec(memory_space=pltpu.VMEM)
SMEM = pl.BlockSpec(memory_space=pltpu.SMEM)


def ahead(array, by):
    return pltpu.roll(array, array.shape[1] - by, 1) if by else array


def window_sum(x):
    two = x + ahead(x, 1)
    four = two + ahead(two, 2)
    eight = four + ahead(four, 4)
    sixteen = eight + ahead(eight, 8)
    half = sixteen + ahead(sixteen, 16)
    full = half + ahead(half, 32)
    return full + ahead(half, 64) + ahead(four, 96)


def fused_kernel(
    n, samp, factor, owner_ref, offset_ref, record_ref, station_ref, valid_ref, out_ref,
    mine, everyone, chan, rows, raw, tpl, gain, win, part, pair, from_a, from_b,
    send_sem, recv_sem, own_sem, pair_send, pair_recv, a_send, a_recv, b_send, b_recv,
):
    me = lax.axis_index("tm")
    plane = me // GROUP
    base = plane * GROUP
    place = lax.rem(me, GROUP)
    parts = mine.shape[1] // 2
    half = samp // 2
    rows_in = SHIFTS * parts
    steps = WIN // SHIFTS
    count = owner_ref.shape[0]
    total = n * samp

    def remote(src, dst, send, recv, to):
        return pltpu.make_async_remote_copy(
            src_ref=src, dst_ref=dst, send_sem=send, recv_sem=recv,
            device_id={"tm": to}, device_id_type=MESH,
        )

    barrier = pltpu.get_barrier_semaphore()

    def greet(d, carry):
        pl.semaphore_signal(
            barrier, inc=1, device_id={"tm": lax.rem(me + d, n)}, device_id_type=MESH
        )
        return carry

    lax.fori_loop(1, n, greet, 0)
    for g in range(GROUP):
        block = record_ref[pl.ds(g * parts, parts), :]
        mine[g] = jnp.concatenate([block[:, :half], block[:, half:]], axis=0).astype(jnp.bfloat16)
    own = pltpu.make_async_copy(mine.at[place], everyone.at[me], own_sem)
    own.start()
    pl.semaphore_wait(barrier, n - 1)

    def target(d):
        return lax.rem(base + (d // GROUP) * GROUP + lax.rem(place + d, GROUP), n)

    def send(d, carry):
        to = target(d)
        remote(
            mine.at[lax.rem(to, GROUP)], everyone.at[me], send_sem.at[d], recv_sem.at[me], to
        ).start()
        return carry

    lax.fori_loop(1, n, send, 0)

    wide = station_ref.shape[1]
    lane = lax.broadcasted_iota(jnp.int32, (parts, wide), 1)
    row = lax.broadcasted_iota(jnp.int32, (parts, wide), 0)
    first_channel = lax.axis_index("sta") * (GROUP * parts) + place * parts
    here = lane == row + first_channel
    stations = station_ref[...].astype(jnp.float32)
    present = valid_ref[...].astype(jnp.float32)
    own_station = jnp.sum(jnp.where(here, stations, 0.0), axis=1, keepdims=True)
    own_valid = jnp.sum(jnp.where(here, present, 0.0), axis=1, keepdims=True)
    counts = jnp.sum(jnp.where(stations == own_station, present, 0.0), axis=1, keepdims=True)
    weight = own_valid / jnp.maximum(counts, 1.0)

    chan[:, pl.ds(total, TAIL)] = jnp.zeros((parts, TAIL), jnp.float32)

    def spread(j):
        block = everyone[j].astype(jnp.float32)
        chan[:, pl.ds(pl.multiple_of(j * samp, samp), half)] = block[:parts]
        chan[:, pl.ds(pl.multiple_of(j * samp + half, half), half)] = block[parts:]

    def arrived(j):
        remote(mine.at[0], everyone.at[j], send_sem.at[0], recv_sem.at[j], j).wait_recv()

    def turn(at, length):
        values = chan[:, pl.ds(at, length + LANES)]
        pieces = [ahead(values, k)[:, :length] for k in range(SHIFTS)]
        pieces.append(jnp.zeros((LANES - rows_in, length), jnp.float32))
        rows[pl.ds(at, length), :] = jnp.concatenate(pieces, axis=0).T

    own.wait()
    spread(me)

    def take_plane(d, carry):
        source = base + lax.rem(place + d, GROUP)
        arrived(source)
        spread(source)
        return carry

    lax.fori_loop(1, GROUP, take_plane, 0)
    after = lax.rem(base + GROUP, n)
    arrived(after)
    spread(after)
    first = pl.multiple_of(base * samp, samp)

    def turn_own(i, carry):
        turn(pl.multiple_of(first + i * samp, samp), samp)
        return carry

    lax.fori_loop(0, GROUP, turn_own, 0)
    turn(pl.multiple_of(first + GROUP * samp, samp), LANES)
    sub = 64

    def window(i, carry):
        at_block = pl.multiple_of(first + i * samp, samp)
        values = chan[:, pl.ds(at_block, samp + LANES)]
        a = window_sum(values)[:, :samp] / WIN
        q = window_sum(values * values)[:, :samp] / WIN
        inverse = 1.0 / jnp.sqrt(jnp.maximum(q - a * a, 0.0) + EPSILON)
        g = weight * inverse
        gain[...] = jnp.concatenate(
            [g] * SHIFTS + [jnp.zeros((LANES - rows_in, samp), jnp.float32)], axis=0
        ).T

        def fill(r, inner):
            at = pl.multiple_of(r * sub, sub)
            scaled = gain[pl.ds(at, sub), :]
            for j in range(steps):
                x = rows[pl.ds(at_block + at + j * SHIFTS, sub), :]
                win[i, pl.ds(at, sub), pl.ds(j * LANES, LANES)] = (x * scaled).astype(jnp.bfloat16)
            return inner

        lax.fori_loop(0, samp // sub, fill, 0)
        return carry

    lax.fori_loop(0, GROUP, window, 0)

    def take_far(e, carry):
        source = lax.rem(base + e, n)
        arrived(source)
        spread(source)
        turn(pl.multiple_of(lax.rem(base + e - 1, n) * samp, samp), samp)
        return carry

    lax.fori_loop(GROUP + 1, n, take_far, 0)
    turn(pl.multiple_of(lax.rem(base + n - 1, n) * samp, samp), samp)
    rows[pl.ds(total, LANES), :] = jnp.zeros((LANES, LANES), jnp.float32)

    def pick(t, carry):
        start = owner_ref[t] * samp + offset_ref[t]
        raw[pl.ds(t, 24, stride=count), :] = rows[pl.ds(start, 24, stride=SHIFTS), :]
        return carry

    lax.fori_loop(0, count, pick, 0)
    lane_a = lax.broadcasted_iota(jnp.int32, (LANES, LANES), 0)
    lane_b = lax.broadcasted_iota(jnp.int32, (LANES, LANES), 1)
    same = (lax.rem(lane_a, parts) == lax.rem(lane_b, parts)) & (
        (lane_a < rows_in) & (lane_b < rows_in)
    )
    fold = jnp.where(same, 1.0, 0.0).astype(jnp.float32)

    def folded(x):
        return jnp.dot(
            x, fold, precision=lax.Precision.HIGHEST, preferred_element_type=jnp.float32
        )

    sums = raw[pl.ds(0, count), :]
    for j in range(1, steps):
        sums = sums + raw[pl.ds(j * count, count), :]
    mean = folded(sums) / WIN
    square = jnp.zeros_like(mean)
    for j in range(steps):
        centred = raw[pl.ds(j * count, count), :] - mean
        square = square + centred * centred
    spread_of = jnp.sqrt(folded(square) / WIN + EPSILON)
    scale = 1.0 / (WIN * spread_of)
    for j in range(steps):
        value = (raw[pl.ds(j * count, count), :] - mean) * scale
        tpl[pl.ds(0, count), pl.ds(j * LANES, LANES)] = value.astype(jnp.bfloat16)
    tpl[pl.ds(count, LANES - count), :] = jnp.zeros(
        (LANES - count, tpl.shape[1]), jnp.bfloat16
    )

    core, x, y = lax.rem(place, 2), lax.rem(place // 2, 2), place // 4
    xa, ya = x + (1 - 2 * x) * (1 - core), y + (1 - 2 * y) * core
    xb, yb = x + (1 - 2 * x) * core, y + (1 - 2 * y) * (1 - core)
    own_chip, chip_a, chip_b = y * 2 + x, ya * 2 + xa, yb * 2 + xb
    diagonal = (1 - y) * 2 + (1 - x)
    mine_order = [diagonal, chip_a, chip_b, own_chip]
    pair_order = [diagonal, chip_b, chip_a, own_chip]
    to_pair = base + own_chip * 2 + (1 - core)
    to_a = base + chip_a * 2 + core
    to_b = base + chip_b * 2 + core
    pair_copies, a_copies, b_copies = [], [], []

    def join(q):
        pair_copies[q].wait_recv()
        part[q, 1] += pair[q]

    for q in range(4):
        block_pair = pair_order[q] * 2 + (1 - core)
        block_mine = mine_order[q] * 2 + core

        def multiply(h, carry, q=q, block_pair=block_pair, block_mine=block_mine):
            block = block_pair + h * (block_mine - block_pair)
            product = lax.dot_general(
                win[block], tpl[...], (((1,), (1,)), ((), ())),
                preferred_element_type=jnp.float32,
            )
            part[q, h] = product.T[:count] * factor
            return carry

        lax.fori_loop(0, 2, multiply, 0)
        copy = remote(part.at[q, 0], pair.at[q], pair_send.at[q], pair_recv.at[q], to_pair)
        copy.start()
        pair_copies.append(copy)
        if q:
            join(q - 1)
        if q in (1, 2):
            copy = remote(
                part.at[q - 1, 1], from_a.at[q - 1], a_send.at[q - 1], a_recv.at[q - 1], to_a
            )
            copy.start()
            a_copies.append(copy)
        if q == 3:
            a_copies[0].wait_recv()
            part[2, 1] += from_a[0]
            copy = remote(part.at[2, 1], from_b, b_send, b_recv, to_b)
            copy.start()
            b_copies.append(copy)
    join(3)
    a_copies[1].wait_recv()
    part[3, 1] += from_a[1]
    b_copies[0].wait_recv()
    out_ref[...] = part[3, 1] + from_b[...]
    for copy in pair_copies + a_copies + b_copies:
        copy.wait_send()

    def sent(d, carry):
        remote(
            mine.at[0], everyone.at[me], send_sem.at[d], recv_sem.at[me], target(d)
        ).wait_send()
        return carry

    lax.fori_loop(1, n, sent, 0)


def body(record, owner, offset, station, valid):
    ch_dev, samp = record.shape
    n = lax.axis_size("tm")
    parts = ch_dev // GROUP
    count = offset.shape[0]
    total = n * samp
    deep = WIN // SHIFTS * LANES
    stations = ch_dev * lax.axis_size("sta") // 3
    station = lax.all_gather(station, "sta", axis=0, tiled=True)
    valid = lax.all_gather(valid, "sta", axis=0, tiled=True)
    dma = pltpu.SemaphoreType.DMA
    f32, bf16 = jnp.float32, jnp.bfloat16
    stack = pl.pallas_call(
        functools.partial(fused_kernel, n, samp, 1.0 / math.sqrt(stations)),
        out_shape=jax.ShapeDtypeStruct((count, samp), f32),
        in_specs=[SMEM, SMEM, VMEM, VMEM, VMEM],
        out_specs=VMEM,
        scratch_shapes=[
            pltpu.VMEM((GROUP, 2 * parts, samp // 2), bf16),
            pltpu.VMEM((n, 2 * parts, samp // 2), bf16),
            pltpu.VMEM((parts, total + TAIL), f32),
            pltpu.VMEM((total + LANES, LANES), f32),
            pltpu.VMEM((24 * count, LANES), f32),
            pltpu.VMEM((LANES, deep), bf16),
            pltpu.VMEM((samp, LANES), f32),
            pltpu.VMEM((GROUP, samp, deep), bf16),
            pltpu.VMEM((4, 2, count, samp), f32),
            pltpu.VMEM((4, count, samp), f32),
            pltpu.VMEM((2, count, samp), f32),
            pltpu.VMEM((count, samp), f32),
            dma((n,)), dma((n,)), dma,
            dma((4,)), dma((4,)), dma((2,)), dma((2,)), dma, dma,
        ],
        compiler_params=pltpu.CompilerParams(
            collective_id=0, has_side_effects=True, vmem_limit_bytes=56 * 1024 * 1024
        ),
    )(owner.reshape(-1), offset, record, station[None, :], valid[None, :])
    stack = stack.reshape(NSTEP, TPL_STEP, samp)
    return lax.psum_scatter(stack, "sta", scatter_dimension=1, tiled=True)


def solution(mesh):
    placed = (P("sta", "tm"), P(), P(), P("sta"), P("sta"))
    return jax.shard_map(
        body, mesh=mesh, in_specs=placed, out_specs=P(None, "sta", "tm"), check_vma=False
    )
```

```python
import functools
import math

import jax
import jax.numpy as jnp
from jax import lax
from jax.experimental import pallas as pl
from jax.experimental.pallas import tpu as pltpu
from jax.sharding import PartitionSpec as P

WIN = 100
TPL_STEP = 32
NSTEP = 3
EPSILON = 1e-05
GROUP = 8
SHIFTS = 5
LANES = 128
TAIL = 256
MESH = pl.DeviceIdType.MESH
VMEM = pl.BlockSpec(memory_space=pltpu.VMEM)
SMEM = pl.BlockSpec(memory_space=pltpu.SMEM)


def ahead(array, by):
    return pltpu.roll(array, array.shape[1] - by, 1) if by else array


def window_sum(x):
    two = x + ahead(x, 1)
    four = two + ahead(two, 2)
    eight = four + ahead(four, 4)
    sixteen = eight + ahead(eight, 8)
    half = sixteen + ahead(sixteen, 16)
    full = half + ahead(half, 32)
    return full + ahead(half, 64) + ahead(four, 96)


def fused_kernel(
    n, samp, factor, owner_ref, offset_ref, record_ref, station_ref, valid_ref, out_ref,
    mine, everyone, eye, chan, rows, raw, tpl, gain, win, part, pair, from_a, from_b,
    send_sem, recv_sem, own_sem, pair_send, pair_recv, a_send, a_recv, b_send, b_recv,
):
    me = lax.axis_index("tm")
    plane = me // GROUP
    base = plane * GROUP
    place = lax.rem(me, GROUP)
    parts = mine.shape[1] // 2
    half = samp // 2
    rows_in = SHIFTS * parts
    steps = WIN // SHIFTS
    count = owner_ref.shape[0]
    total = n * samp

    def remote(src, dst, send, recv, to):
        return pltpu.make_async_remote_copy(
            src_ref=src, dst_ref=dst, send_sem=send, recv_sem=recv,
            device_id={"tm": to}, device_id_type=MESH,
        )

    barrier = pltpu.get_barrier_semaphore()

    def greet(d, carry):
        pl.semaphore_signal(
            barrier, inc=1, device_id={"tm": lax.rem(me + d, n)}, device_id_type=MESH
        )
        return carry

    lax.fori_loop(1, n, greet, 0)
    for g in range(GROUP):
        block = record_ref[pl.ds(g * parts, parts), :]
        mine[g] = jnp.concatenate([block[:, :half], block[:, half:]], axis=0).astype(jnp.bfloat16)
    own = pltpu.make_async_copy(mine.at[place], everyone.at[me], own_sem)
    own.start()
    pl.semaphore_wait(barrier, n - 1)

    def target(d):
        return lax.rem(base + n - (d // GROUP) * GROUP + lax.rem(place + d, GROUP), n)

    def send(d, carry):
        to = target(d)
        remote(
            mine.at[lax.rem(to, GROUP)], everyone.at[me], send_sem.at[d], recv_sem.at[me], to
        ).start()
        return carry

    lax.fori_loop(1, n, send, 0)

    wide = station_ref.shape[1]
    lane = lax.broadcasted_iota(jnp.int32, (parts, wide), 1)
    row = lax.broadcasted_iota(jnp.int32, (parts, wide), 0)
    first_channel = lax.axis_index("sta") * (GROUP * parts) + place * parts
    here = lane == row + first_channel
    stations = station_ref[...].astype(jnp.float32)
    present = valid_ref[...].astype(jnp.float32)
    own_station = jnp.sum(jnp.where(here, stations, 0.0), axis=1, keepdims=True)
    own_valid = jnp.sum(jnp.where(here, present, 0.0), axis=1, keepdims=True)
    counts = jnp.sum(jnp.where(stations == own_station, present, 0.0), axis=1, keepdims=True)
    weight = own_valid / jnp.maximum(counts, 1.0)

    eye[...] = jnp.where(
        lax.broadcasted_iota(jnp.int32, eye.shape, 0) == lax.broadcasted_iota(jnp.int32, eye.shape, 1),
        1.0, 0.0,
    ).astype(jnp.bfloat16)
    chan[:, pl.ds(total, TAIL)] = jnp.zeros((parts, TAIL), jnp.float32)

    def spread(j):
        block = everyone[j].astype(jnp.float32)
        chan[:, pl.ds(pl.multiple_of(j * samp, samp), half)] = block[:parts]
        chan[:, pl.ds(pl.multiple_of(j * samp + half, half), half)] = block[parts:]

    def arrived(j):
        remote(mine.at[0], everyone.at[j], send_sem.at[0], recv_sem.at[j], j).wait_recv()

    def turn(at, length):
        values = chan[:, pl.ds(at, length + LANES)]
        pieces = [ahead(values, k)[:, :length] for k in range(SHIFTS)]
        pieces.append(jnp.zeros((LANES - rows_in, length), jnp.float32))
        wide_rows = jnp.concatenate(pieces, axis=0).astype(jnp.bfloat16)
        for cut in range(0, length, 2 * LANES):
            size = min(2 * LANES, length - cut)
            rows[pl.ds(at + cut, size), :] = lax.dot_general(
                eye[pl.ds(0, size), pl.ds(0, size)], wide_rows[:, cut : cut + size],
                (((1,), (1,)), ((), ())), preferred_element_type=jnp.float32,
            )

    own.wait()
    spread(me)

    def take_plane(d, carry):
        source = base + lax.rem(place + d, GROUP)
        arrived(source)
        spread(source)
        return carry

    lax.fori_loop(1, GROUP, take_plane, 0)
    first = pl.multiple_of(base * samp, samp)

    def turn_own(i, carry):
        turn(pl.multiple_of(first + i * samp, samp), samp)
        return carry

    lax.fori_loop(0, GROUP - 1, turn_own, 0)
    sub = 64

    def window(i, carry):
        at_block = pl.multiple_of(first + i * samp, samp)
        values = chan[:, pl.ds(at_block, samp + LANES)]
        a = window_sum(values)[:, :samp] / WIN
        q = window_sum(values * values)[:, :samp] / WIN
        inverse = 1.0 / jnp.sqrt(jnp.maximum(q - a * a, 0.0) + EPSILON)
        g = weight * inverse
        gain[...] = jnp.concatenate(
            [g] * SHIFTS + [jnp.zeros((LANES - rows_in, samp), jnp.float32)], axis=0
        ).T

        def fill(r, inner):
            at = pl.multiple_of(r * sub, sub)
            scaled = gain[pl.ds(at, sub), :]
            for j in range(steps):
                x = rows[pl.ds(at_block + at + j * SHIFTS, sub), :]
                win[i, pl.ds(at, sub), pl.ds(j * LANES, LANES)] = (x * scaled).astype(jnp.bfloat16)
            return inner

        lax.fori_loop(0, samp // sub, fill, 0)
        return carry

    lax.fori_loop(0, GROUP - 2, window, 0)
    after = lax.rem(base + GROUP, n)
    arrived(after)
    spread(after)
    turn_own(GROUP - 1, 0)
    turn(pl.multiple_of(first + GROUP * samp, samp), LANES)
    lax.fori_loop(GROUP - 2, GROUP, window, 0)

    def take_far(e, carry):
        source = lax.rem(base + e, n)
        arrived(source)
        spread(source)
        turn(pl.multiple_of(lax.rem(base + e - 1, n) * samp, samp), samp)
        return carry

    lax.fori_loop(GROUP + 1, n, take_far, 0)
    turn(pl.multiple_of(lax.rem(base + n - 1, n) * samp, samp), samp)
    rows[pl.ds(total, LANES), :] = jnp.zeros((LANES, LANES), jnp.float32)

    def pick(b, carry):
        found = []
        for t in range(8):
            start = owner_ref[b * 8 + t] * samp + offset_ref[b * 8 + t]
            found.append(rows[pl.ds(start, 24, stride=SHIFTS), :])
        for t in range(8):
            raw[pl.ds(b * 8 + t, 24, stride=count), :] = found[t]
        return carry

    lax.fori_loop(0, count // 8, pick, 0)
    lane_a = lax.broadcasted_iota(jnp.int32, (LANES, LANES), 0)
    lane_b = lax.broadcasted_iota(jnp.int32, (LANES, LANES), 1)
    same = (lax.rem(lane_a, parts) == lax.rem(lane_b, parts)) & (
        (lane_a < rows_in) & (lane_b < rows_in)
    )
    fold = jnp.where(same, 1.0, 0.0).astype(jnp.float32)

    def folded(x):
        return jnp.dot(
            x, fold, precision=lax.Precision.HIGHEST, preferred_element_type=jnp.float32
        )

    sums = raw[pl.ds(0, count), :]
    for j in range(1, steps):
        sums = sums + raw[pl.ds(j * count, count), :]
    mean = folded(sums) / WIN
    square = jnp.zeros_like(mean)
    for j in range(steps):
        centred = raw[pl.ds(j * count, count), :] - mean
        square = square + centred * centred
    spread_of = jnp.sqrt(folded(square) / WIN + EPSILON)
    scale = 1.0 / (WIN * spread_of)
    for j in range(steps):
        value = (raw[pl.ds(j * count, count), :] - mean) * scale
        tpl[pl.ds(0, count), pl.ds(j * LANES, LANES)] = value.astype(jnp.bfloat16)
    tpl[pl.ds(count, LANES - count), :] = jnp.zeros(
        (LANES - count, tpl.shape[1]), jnp.bfloat16
    )

    core, x, y = lax.rem(place, 2), lax.rem(place // 2, 2), place // 4
    xa, ya = x + (1 - 2 * x) * (1 - core), y + (1 - 2 * y) * core
    xb, yb = x + (1 - 2 * x) * core, y + (1 - 2 * y) * (1 - core)
    own_chip, chip_a, chip_b = y * 2 + x, ya * 2 + xa, yb * 2 + xb
    diagonal = (1 - y) * 2 + (1 - x)
    mine_order = [diagonal, chip_a, chip_b, own_chip]
    pair_order = [diagonal, chip_b, chip_a, own_chip]
    to_pair = base + own_chip * 2 + (1 - core)
    to_a = base + chip_a * 2 + core
    to_b = base + chip_b * 2 + core
    pair_copies, a_copies, b_copies = [], [], []

    def join(q):
        pair_copies[q].wait_recv()
        part[q, 1] += pair[q]

    for q in range(4):
        block_pair = pair_order[q] * 2 + (1 - core)
        block_mine = mine_order[q] * 2 + core

        def multiply(h, carry, q=q, block_pair=block_pair, block_mine=block_mine):
            block = block_pair + h * (block_mine - block_pair)
            product = lax.dot_general(
                win[block], tpl[...], (((1,), (1,)), ((), ())),
                preferred_element_type=jnp.float32,
            )
            part[q, h] = product.T[:count] * factor
            return carry

        lax.fori_loop(0, 2, multiply, 0)
        copy = remote(part.at[q, 0], pair.at[q], pair_send.at[q], pair_recv.at[q], to_pair)
        copy.start()
        pair_copies.append(copy)
        if q:
            join(q - 1)
        if q in (1, 2):
            copy = remote(
                part.at[q - 1, 1], from_a.at[q - 1], a_send.at[q - 1], a_recv.at[q - 1], to_a
            )
            copy.start()
            a_copies.append(copy)
        if q == 3:
            a_copies[0].wait_recv()
            part[2, 1] += from_a[0]
            copy = remote(part.at[2, 1], from_b, b_send, b_recv, to_b)
            copy.start()
            b_copies.append(copy)
    join(3)
    a_copies[1].wait_recv()
    part[3, 1] += from_a[1]
    b_copies[0].wait_recv()
    out_ref[...] = part[3, 1] + from_b[...]
    for copy in pair_copies + a_copies + b_copies:
        copy.wait_send()

    def sent(d, carry):
        remote(
            mine.at[0], everyone.at[me], send_sem.at[d], recv_sem.at[me], target(d)
        ).wait_send()
        return carry

    lax.fori_loop(1, n, sent, 0)


def body(record, owner, offset, station, valid):
    ch_dev, samp = record.shape
    n = lax.axis_size("tm")
    parts = ch_dev // GROUP
    count = offset.shape[0]
    total = n * samp
    deep = WIN // SHIFTS * LANES
    stations = ch_dev * lax.axis_size("sta") // 3
    station = lax.all_gather(station, "sta", axis=0, tiled=True)
    valid = lax.all_gather(valid, "sta", axis=0, tiled=True)
    dma = pltpu.SemaphoreType.DMA
    f32, bf16 = jnp.float32, jnp.bfloat16
    stack = pl.pallas_call(
        functools.partial(fused_kernel, n, samp, 1.0 / math.sqrt(stations)),
        out_shape=jax.ShapeDtypeStruct((count, samp), f32),
        in_specs=[SMEM, SMEM, VMEM, VMEM, VMEM],
        out_specs=VMEM,
        scratch_shapes=[
            pltpu.VMEM((GROUP, 2 * parts, samp // 2), bf16),
            pltpu.VMEM((n, 2 * parts, samp // 2), bf16),
            pltpu.VMEM((2 * LANES, 2 * LANES), bf16),
            pltpu.VMEM((parts, total + TAIL), f32),
            pltpu.VMEM((total + LANES, LANES), f32),
            pltpu.VMEM((24 * count, LANES), f32),
            pltpu.VMEM((LANES, deep), bf16),
            pltpu.VMEM((samp, LANES), f32),
            pltpu.VMEM((GROUP, samp, deep), bf16),
            pltpu.VMEM((4, 2, count, samp), f32),
            pltpu.VMEM((4, count, samp), f32),
            pltpu.VMEM((2, count, samp), f32),
            pltpu.VMEM((count, samp), f32),
            dma((n,)), dma((n,)), dma,
            dma((4,)), dma((4,)), dma((2,)), dma((2,)), dma, dma,
        ],
        compiler_params=pltpu.CompilerParams(
            collective_id=0, has_side_effects=True, vmem_limit_bytes=56 * 1024 * 1024
        ),
    )(owner.reshape(-1), offset, record, station[None, :], valid[None, :])
    stack = stack.reshape(NSTEP, TPL_STEP, samp)
    return lax.psum_scatter(stack, "sta", scatter_dimension=1, tiled=True)


def solution(mesh):
    placed = (P("sta", "tm"), P(), P(), P("sta"), P("sta"))
    return jax.shard_map(
        body, mesh=mesh, in_specs=placed, out_specs=P(None, "sta", "tm"), check_vma=False
    )
```

```python
import functools
import math

import jax
import jax.numpy as jnp
from jax import lax
from jax.experimental import pallas as pl
from jax.experimental.pallas import tpu as pltpu
from jax.sharding import PartitionSpec as P

WIN = 100
TPL_STEP = 32
NSTEP = 3
EPSILON = 1e-05
GROUP = 8
SHIFTS = 5
LANES = 128
TAIL = 256
MESH = pl.DeviceIdType.MESH
VMEM = pl.BlockSpec(memory_space=pltpu.VMEM)
SMEM = pl.BlockSpec(memory_space=pltpu.SMEM)


def ahead(array, by):
    return pltpu.roll(array, array.shape[1] - by, 1) if by else array


def window_sum(x):
    two = x + ahead(x, 1)
    four = two + ahead(two, 2)
    eight = four + ahead(four, 4)
    sixteen = eight + ahead(eight, 8)
    half = sixteen + ahead(sixteen, 16)
    full = half + ahead(half, 32)
    return full + ahead(half, 64) + ahead(four, 96)


def fused_kernel(
    n, samp, factor, owner_ref, offset_ref, record_ref, station_ref, valid_ref, out_ref,
    mine, everyone, eye, chan, rows, raw, tpl, gain, win, part, pair, from_a, from_b,
    send_sem, recv_sem, own_sem, pair_send, pair_recv, a_send, a_recv, b_send, b_recv,
):
    me = lax.axis_index("tm")
    plane = me // GROUP
    base = plane * GROUP
    place = lax.rem(me, GROUP)
    parts = mine.shape[1] // 2
    half = samp // 2
    rows_in = SHIFTS * parts
    steps = WIN // SHIFTS
    count = owner_ref.shape[0]
    total = n * samp

    def remote(src, dst, send, recv, to):
        return pltpu.make_async_remote_copy(
            src_ref=src, dst_ref=dst, send_sem=send, recv_sem=recv,
            device_id={"tm": to}, device_id_type=MESH,
        )

    barrier = pltpu.get_barrier_semaphore()

    def greet(d, carry):
        pl.semaphore_signal(
            barrier, inc=1, device_id={"tm": lax.rem(me + d, n)}, device_id_type=MESH
        )
        return carry

    lax.fori_loop(1, n, greet, 0)
    for g in range(GROUP):
        block = record_ref[pl.ds(g * parts, parts), :]
        mine[g] = jnp.concatenate([block[:, :half], block[:, half:]], axis=0).astype(jnp.bfloat16)
    own = pltpu.make_async_copy(mine.at[place], everyone.at[me], own_sem)
    own.start()
    pl.semaphore_wait(barrier, n - 1)

    def target(d):
        return lax.rem(base + n - (d // GROUP) * GROUP + lax.rem(place + d, GROUP), n)

    def send(d, carry):
        to = target(d)
        remote(
            mine.at[lax.rem(to, GROUP)], everyone.at[me], send_sem.at[d], recv_sem.at[me], to
        ).start()
        return carry

    lax.fori_loop(1, n, send, 0)

    wide = station_ref.shape[1]
    lane = lax.broadcasted_iota(jnp.int32, (parts, wide), 1)
    row = lax.broadcasted_iota(jnp.int32, (parts, wide), 0)
    first_channel = lax.axis_index("sta") * (GROUP * parts) + place * parts
    here = lane == row + first_channel
    stations = station_ref[...].astype(jnp.float32)
    present = valid_ref[...].astype(jnp.float32)
    own_station = jnp.sum(jnp.where(here, stations, 0.0), axis=1, keepdims=True)
    own_valid = jnp.sum(jnp.where(here, present, 0.0), axis=1, keepdims=True)
    counts = jnp.sum(jnp.where(stations == own_station, present, 0.0), axis=1, keepdims=True)
    weight = own_valid / jnp.maximum(counts, 1.0)

    eye[...] = jnp.where(
        lax.broadcasted_iota(jnp.int32, eye.shape, 0) == lax.broadcasted_iota(jnp.int32, eye.shape, 1),
        1.0, 0.0,
    ).astype(jnp.bfloat16)
    chan[:, pl.ds(total, TAIL)] = jnp.zeros((parts, TAIL), jnp.float32)

    def spread(j):
        block = everyone[j].astype(jnp.float32)
        chan[:, pl.ds(pl.multiple_of(j * samp, samp), half)] = block[:parts]
        chan[:, pl.ds(pl.multiple_of(j * samp + half, half), half)] = block[parts:]

    def arrived(j):
        remote(mine.at[0], everyone.at[j], send_sem.at[0], recv_sem.at[j], j).wait_recv()

    def turn(at, length):
        values = chan[:, pl.ds(at, length + LANES)]
        pieces = [ahead(values, k)[:, :length] for k in range(SHIFTS)]
        pieces.append(jnp.zeros((LANES - rows_in, length), jnp.float32))
        wide_rows = jnp.concatenate(pieces, axis=0).astype(jnp.bfloat16)
        for cut in range(0, length, 2 * LANES):
            size = min(2 * LANES, length - cut)
            rows[pl.ds(at + cut, size), :] = lax.dot_general(
                eye[pl.ds(0, size), pl.ds(0, size)], wide_rows[:, cut : cut + size],
                (((1,), (1,)), ((), ())), preferred_element_type=jnp.float32,
            )

    own.wait()
    spread(me)

    def take_plane(d, carry):
        source = base + lax.rem(place + d, GROUP)
        arrived(source)
        spread(source)
        return carry

    lax.fori_loop(1, GROUP, take_plane, 0)
    first = pl.multiple_of(base * samp, samp)

    for i in range(GROUP - 1):
        turn(pl.multiple_of(first + i * samp, samp), samp)
    sub = 64

    def gains(at, length):
        values = chan[:, pl.ds(at, length + LANES)]
        a = window_sum(values)[:, :length] / WIN
        q = window_sum(values * values)[:, :length] / WIN
        inverse = 1.0 / jnp.sqrt(jnp.maximum(q - a * a, 0.0) + EPSILON)
        g = weight * inverse
        zeros = jnp.zeros((LANES - rows_in, length), jnp.float32)
        gain[pl.ds(pl.multiple_of(at - first, samp), length), :] = jnp.concatenate(
            [g] * SHIFTS + [zeros], axis=0
        ).T

    def gains_two(i, carry):
        gains(pl.multiple_of(first + i * (2 * samp), samp), 2 * samp)
        return carry

    def fill(r, carry):
        at = pl.multiple_of(r * sub, sub)
        scaled = gain[pl.ds(at, sub), :]
        for j in range(steps):
            x = rows[pl.ds(first + at + j * SHIFTS, sub), :]
            win[pl.ds(at, sub), pl.ds(j * LANES, LANES)] = (x * scaled).astype(jnp.bfloat16)
        return carry

    early = (GROUP - 2) * samp // sub
    lax.fori_loop(0, GROUP // 2 - 1, gains_two, 0)
    lax.fori_loop(0, early, fill, 0)
    after = lax.rem(base + GROUP, n)
    arrived(after)
    spread(after)
    turn(pl.multiple_of(first + (GROUP - 1) * samp, samp), samp)
    turn(pl.multiple_of(first + GROUP * samp, samp), LANES)
    gains_two(GROUP // 2 - 1, 0)
    lax.fori_loop(early, GROUP * samp // sub, fill, 0)

    def take_far(e, blocks):
        for d in range(blocks):
            source = lax.rem(base + e + d, n)
            arrived(source)
            spread(source)
        for d in range(4):
            turn(pl.multiple_of(lax.rem(base + e + d - 1, n) * samp, samp), samp)

    def take_four(i, carry):
        take_far(GROUP + 1 + i * 4, 4)
        return carry

    far = n - GROUP - 1
    lax.fori_loop(0, far // 4, take_four, 0)
    take_far(n - far % 4, far % 4)
    rows[pl.ds(total, LANES), :] = jnp.zeros((LANES, LANES), jnp.float32)

    def pick(b, carry):
        found = []
        for t in range(8):
            start = owner_ref[b * 8 + t] * samp + offset_ref[b * 8 + t]
            found.append(rows[pl.ds(start, 24, stride=SHIFTS), :])
        for t in range(8):
            raw[pl.ds(b * 8 + t, 24, stride=count), :] = found[t]
        return carry

    lax.fori_loop(0, count // 8, pick, 0)
    lane_a = lax.broadcasted_iota(jnp.int32, (LANES, LANES), 0)
    lane_b = lax.broadcasted_iota(jnp.int32, (LANES, LANES), 1)
    same = (lax.rem(lane_a, parts) == lax.rem(lane_b, parts)) & (
        (lane_a < rows_in) & (lane_b < rows_in)
    )
    fold = jnp.where(same, 1.0, 0.0).astype(jnp.float32)

    def folded(x):
        return jnp.dot(
            x, fold, precision=lax.Precision.HIGHEST, preferred_element_type=jnp.float32
        )

    sums = raw[pl.ds(0, count), :]
    for j in range(1, steps):
        sums = sums + raw[pl.ds(j * count, count), :]
    mean = folded(sums) / WIN
    square = jnp.zeros_like(mean)
    for j in range(steps):
        centred = raw[pl.ds(j * count, count), :] - mean
        square = square + centred * centred
    spread_of = jnp.sqrt(folded(square) / WIN + EPSILON)
    scale = 1.0 / (WIN * spread_of)
    for j in range(steps):
        value = (raw[pl.ds(j * count, count), :] - mean) * scale
        tpl[pl.ds(0, count), pl.ds(j * LANES, LANES)] = value.astype(jnp.bfloat16)
    tpl[pl.ds(count, LANES - count), :] = jnp.zeros(
        (LANES - count, tpl.shape[1]), jnp.bfloat16
    )

    core, x, y = lax.rem(place, 2), lax.rem(place // 2, 2), place // 4
    xa, ya = x + (1 - 2 * x) * (1 - core), y + (1 - 2 * y) * core
    xb, yb = x + (1 - 2 * x) * core, y + (1 - 2 * y) * (1 - core)
    own_chip, chip_a, chip_b = y * 2 + x, ya * 2 + xa, yb * 2 + xb
    diagonal = (1 - y) * 2 + (1 - x)
    mine_order = [diagonal, chip_a, chip_b, own_chip]
    pair_order = [diagonal, chip_b, chip_a, own_chip]
    to_pair = base + own_chip * 2 + (1 - core)
    to_a = base + chip_a * 2 + core
    to_b = base + chip_b * 2 + core
    pair_copies, a_copies, b_copies = [], [], []

    def join(q):
        pair_copies[q].wait_recv()
        part[q, 1] += pair[q]

    for q in range(4):
        block_pair = pair_order[q] * 2 + (1 - core)
        block_mine = mine_order[q] * 2 + core

        for h, block in ((0, block_pair), (1, block_mine)):
            product = lax.dot_general(
                win[pl.ds(pl.multiple_of(block * samp, samp), samp), :], tpl[...],
                (((1,), (1,)), ((), ())), preferred_element_type=jnp.float32,
            )
            part[q, h] = product.T[:count] * factor
        copy = remote(part.at[q, 0], pair.at[q], pair_send.at[q], pair_recv.at[q], to_pair)
        copy.start()
        pair_copies.append(copy)
        if q:
            join(q - 1)
        if q in (1, 2):
            copy = remote(
                part.at[q - 1, 1], from_a.at[q - 1], a_send.at[q - 1], a_recv.at[q - 1], to_a
            )
            copy.start()
            a_copies.append(copy)
        if q == 3:
            a_copies[0].wait_recv()
            part[2, 1] += from_a[0]
            copy = remote(part.at[2, 1], from_b, b_send, b_recv, to_b)
            copy.start()
            b_copies.append(copy)
    join(3)
    a_copies[1].wait_recv()
    part[3, 1] += from_a[1]
    b_copies[0].wait_recv()
    out_ref[...] = part[3, 1] + from_b[...]
    for copy in pair_copies + a_copies + b_copies:
        copy.wait_send()

    def sent(d, carry):
        remote(
            mine.at[0], everyone.at[me], send_sem.at[d], recv_sem.at[me], target(d)
        ).wait_send()
        return carry

    lax.fori_loop(1, n, sent, 0)


def body(record, owner, offset, station, valid):
    ch_dev, samp = record.shape
    n = lax.axis_size("tm")
    parts = ch_dev // GROUP
    count = offset.shape[0]
    total = n * samp
    deep = WIN // SHIFTS * LANES
    stations = ch_dev * lax.axis_size("sta") // 3
    station = lax.all_gather(station, "sta", axis=0, tiled=True)
    valid = lax.all_gather(valid, "sta", axis=0, tiled=True)
    dma = pltpu.SemaphoreType.DMA
    f32, bf16 = jnp.float32, jnp.bfloat16
    stack = pl.pallas_call(
        functools.partial(fused_kernel, n, samp, 1.0 / math.sqrt(stations)),
        out_shape=jax.ShapeDtypeStruct((count, samp), f32),
        in_specs=[SMEM, SMEM, VMEM, VMEM, VMEM],
        out_specs=VMEM,
        scratch_shapes=[
            pltpu.VMEM((GROUP, 2 * parts, samp // 2), bf16),
            pltpu.VMEM((n, 2 * parts, samp // 2), bf16),
            pltpu.VMEM((2 * LANES, 2 * LANES), bf16),
            pltpu.VMEM((parts, total + TAIL), f32),
            pltpu.VMEM((total + LANES, LANES), f32),
            pltpu.VMEM((24 * count, LANES), f32),
            pltpu.VMEM((LANES, deep), bf16),
            pltpu.VMEM((GROUP * samp, LANES), f32),
            pltpu.VMEM((GROUP * samp, deep), bf16),
            pltpu.VMEM((4, 2, count, samp), f32),
            pltpu.VMEM((4, count, samp), f32),
            pltpu.VMEM((2, count, samp), f32),
            pltpu.VMEM((count, samp), f32),
            dma((n,)), dma((n,)), dma,
            dma((4,)), dma((4,)), dma((2,)), dma((2,)), dma, dma,
        ],
        compiler_params=pltpu.CompilerParams(
            collective_id=0, has_side_effects=True, vmem_limit_bytes=56 * 1024 * 1024
        ),
    )(owner.reshape(-1), offset, record, station[None, :], valid[None, :])
    stack = stack.reshape(NSTEP, TPL_STEP, samp)
    return lax.psum_scatter(stack, "sta", scatter_dimension=1, tiled=True)


def solution(mesh):
    placed = (P("sta", "tm"), P(), P(), P("sta"), P("sta"))
    return jax.shard_map(
        body, mesh=mesh, in_specs=placed, out_specs=P(None, "sta", "tm"), check_vma=False
    )
```

```python
import functools
import math

import jax
import jax.numpy as jnp
from jax import lax
from jax.experimental import pallas as pl
from jax.experimental.pallas import tpu as pltpu
from jax.sharding import PartitionSpec as P

WIN = 100
TPL_STEP = 32
NSTEP = 3
EPSILON = 1e-05
GROUP = 8
SHIFTS = 5
LANES = 128
TAIL = 256
MESH = pl.DeviceIdType.MESH
VMEM = pl.BlockSpec(memory_space=pltpu.VMEM)
SMEM = pl.BlockSpec(memory_space=pltpu.SMEM)


def ahead(array, by):
    return pltpu.roll(array, array.shape[1] - by, 1) if by else array


def window_sum(x):
    two = x + ahead(x, 1)
    four = two + ahead(two, 2)
    eight = four + ahead(four, 4)
    sixteen = eight + ahead(eight, 8)
    half = sixteen + ahead(sixteen, 16)
    full = half + ahead(half, 32)
    return full + ahead(half, 64) + ahead(four, 96)


def fused_kernel(
    n, samp, factor, owner_ref, offset_ref, record_ref, station_ref, valid_ref, out_ref,
    mine, everyone, eye, chan, rows, raw, tpl, gain, win, part, pair, from_a, from_b,
    send_sem, recv_sem, own_sem, pair_send, pair_recv, a_send, a_recv, b_send, b_recv,
):
    me = lax.axis_index("tm")
    plane = me // GROUP
    base = plane * GROUP
    place = lax.rem(me, GROUP)
    parts = mine.shape[1] // 2
    half = samp // 2
    rows_in = SHIFTS * parts
    steps = WIN // SHIFTS
    count = owner_ref.shape[0]
    total = n * samp

    def remote(src, dst, send, recv, to):
        return pltpu.make_async_remote_copy(
            src_ref=src, dst_ref=dst, send_sem=send, recv_sem=recv,
            device_id={"tm": to}, device_id_type=MESH,
        )

    barrier = pltpu.get_barrier_semaphore()

    def greet(d, carry):
        pl.semaphore_signal(
            barrier, inc=1, device_id={"tm": lax.rem(me + d, n)}, device_id_type=MESH
        )
        return carry

    lax.fori_loop(1, n, greet, 0)
    for g in range(GROUP):
        block = record_ref[pl.ds(g * parts, parts), :]
        mine[g] = jnp.concatenate([block[:, :half], block[:, half:]], axis=0).astype(jnp.bfloat16)
    own = pltpu.make_async_copy(mine.at[place], everyone.at[me], own_sem)
    own.start()
    pl.semaphore_wait(barrier, n - 1)

    def target(d):
        return lax.rem(base + n - (d // GROUP) * GROUP + lax.rem(place + d, GROUP), n)

    def send(d, carry):
        to = target(d)
        remote(
            mine.at[lax.rem(to, GROUP)], everyone.at[me], send_sem.at[d], recv_sem.at[me], to
        ).start()
        return carry

    lax.fori_loop(1, n, send, 0)

    wide = station_ref.shape[1]
    lane = lax.broadcasted_iota(jnp.int32, (parts, wide), 1)
    row = lax.broadcasted_iota(jnp.int32, (parts, wide), 0)
    first_channel = lax.axis_index("sta") * (GROUP * parts) + place * parts
    here = lane == row + first_channel
    stations = station_ref[...].astype(jnp.float32)
    present = valid_ref[...].astype(jnp.float32)
    own_station = jnp.sum(jnp.where(here, stations, 0.0), axis=1, keepdims=True)
    own_valid = jnp.sum(jnp.where(here, present, 0.0), axis=1, keepdims=True)
    counts = jnp.sum(jnp.where(stations == own_station, present, 0.0), axis=1, keepdims=True)
    weight = own_valid / jnp.maximum(counts, 1.0)

    eye[...] = jnp.where(
        lax.broadcasted_iota(jnp.int32, eye.shape, 0) == lax.broadcasted_iota(jnp.int32, eye.shape, 1),
        1.0, 0.0,
    ).astype(jnp.bfloat16)
    chan[:, pl.ds(total, TAIL)] = jnp.zeros((parts, TAIL), jnp.float32)

    def spread(j):
        block = everyone[j].astype(jnp.float32)
        chan[:, pl.ds(pl.multiple_of(j * samp, samp), half)] = block[:parts]
        chan[:, pl.ds(pl.multiple_of(j * samp + half, half), half)] = block[parts:]

    def arrived(j):
        remote(mine.at[0], everyone.at[j], send_sem.at[0], recv_sem.at[j], j).wait_recv()

    def turn(at, length):
        values = chan[:, pl.ds(at, length + LANES)]
        pieces = [ahead(values, k)[:, :length] for k in range(SHIFTS)]
        pieces.append(jnp.zeros((LANES - rows_in, length), jnp.float32))
        wide_rows = jnp.concatenate(pieces, axis=0).astype(jnp.bfloat16)
        for cut in range(0, length, 2 * LANES):
            size = min(2 * LANES, length - cut)
            rows[pl.ds(at + cut, size), :] = lax.dot_general(
                eye[pl.ds(0, size), pl.ds(0, size)], wide_rows[:, cut : cut + size],
                (((1,), (1,)), ((), ())), preferred_element_type=jnp.float32,
            )

    own.wait()
    spread(me)

    def take_plane(d, carry):
        source = base + lax.rem(place + d, GROUP)
        arrived(source)
        spread(source)
        return carry

    lax.fori_loop(1, GROUP, take_plane, 0)
    first = pl.multiple_of(base * samp, samp)

    for i in range(GROUP - 1):
        turn(pl.multiple_of(first + i * samp, samp), samp)
    sub = 64

    def gains(at, length):
        values = chan[:, pl.ds(at, length + LANES)]
        a = window_sum(values)[:, :length] / WIN
        q = window_sum(values * values)[:, :length] / WIN
        inverse = 1.0 / jnp.sqrt(jnp.maximum(q - a * a, 0.0) + EPSILON)
        g = weight * inverse
        zeros = jnp.zeros((LANES - rows_in, length), jnp.float32)
        gain[pl.ds(pl.multiple_of(at - first, samp), length), :] = jnp.concatenate(
            [g] * SHIFTS + [zeros], axis=0
        ).T

    def gains_two(i, carry):
        gains(pl.multiple_of(first + i * (2 * samp), samp), 2 * samp)
        return carry

    def fill(r, carry):
        at = pl.multiple_of(r * sub, sub)
        scaled = gain[pl.ds(at, sub), :]
        for j in range(steps):
            x = rows[pl.ds(first + at + j * SHIFTS, sub), :]
            win[pl.ds(at, sub), pl.ds(j * LANES, LANES)] = (x * scaled).astype(jnp.bfloat16)
        return carry

    early = (GROUP - 2) * samp // sub
    lax.fori_loop(0, GROUP // 2 - 1, gains_two, 0)
    lax.fori_loop(0, early, fill, 0)
    after = lax.rem(base + GROUP, n)
    arrived(after)
    spread(after)
    turn(pl.multiple_of(first + (GROUP - 1) * samp, samp), samp)
    turn(pl.multiple_of(first + GROUP * samp, samp), LANES)
    gains_two(GROUP // 2 - 1, 0)
    lax.fori_loop(early, GROUP * samp // sub, fill, 0)

    def take_far(e, blocks):
        for d in range(blocks):
            source = lax.rem(base + e + d, n)
            arrived(source)
            spread(source)
        for d in range(4):
            turn(pl.multiple_of(lax.rem(base + e + d - 1, n) * samp, samp), samp)

    def take_four(i, carry):
        take_far(GROUP + 1 + i * 4, 4)
        return carry

    far = n - GROUP - 1
    lax.fori_loop(0, far // 4, take_four, 0)
    take_far(n - far % 4, far % 4)
    rows[pl.ds(total, LANES), :] = jnp.zeros((LANES, LANES), jnp.float32)

    def pick(b, carry):
        found = []
        for t in range(8):
            start = owner_ref[b * 8 + t] * samp + offset_ref[b * 8 + t]
            found.append(rows[pl.ds(start, 24, stride=SHIFTS), :])
        for t in range(8):
            raw[pl.ds(b * 8 + t, 24, stride=count), :] = found[t]
        return carry

    lax.fori_loop(0, count // 8, pick, 0)
    lane_a = lax.broadcasted_iota(jnp.int32, (LANES, LANES), 0)
    lane_b = lax.broadcasted_iota(jnp.int32, (LANES, LANES), 1)
    same = (lax.rem(lane_a, parts) == lax.rem(lane_b, parts)) & (
        (lane_a < rows_in) & (lane_b < rows_in)
    )
    fold = jnp.where(same, 1.0, 0.0).astype(jnp.float32)

    def folded(x):
        return jnp.dot(
            x, fold, precision=lax.Precision.HIGHEST, preferred_element_type=jnp.float32
        )

    sums = raw[pl.ds(0, count), :]
    for j in range(1, steps):
        sums = sums + raw[pl.ds(j * count, count), :]
    mean = folded(sums) / WIN
    square = jnp.zeros_like(mean)
    for j in range(steps):
        centred = raw[pl.ds(j * count, count), :] - mean
        square = square + centred * centred
    spread_of = jnp.sqrt(folded(square) / WIN + EPSILON)
    scale = 1.0 / (WIN * spread_of)
    for j in range(steps):
        value = (raw[pl.ds(j * count, count), :] - mean) * scale
        tpl[:, pl.ds(j * LANES, LANES)] = value.astype(jnp.bfloat16)

    core, x, y = lax.rem(place, 2), lax.rem(place // 2, 2), place // 4
    xa, ya = x + (1 - 2 * x) * (1 - core), y + (1 - 2 * y) * core
    xb, yb = x + (1 - 2 * x) * core, y + (1 - 2 * y) * (1 - core)
    own_chip, chip_a, chip_b = y * 2 + x, ya * 2 + xa, yb * 2 + xb
    diagonal = (1 - y) * 2 + (1 - x)
    mine_order = [diagonal, chip_a, chip_b, own_chip]
    pair_order = [diagonal, chip_b, chip_a, own_chip]
    to_pair = base + own_chip * 2 + (1 - core)
    to_a = base + chip_a * 2 + core
    to_b = base + chip_b * 2 + core
    pair_copies, a_copies, b_copies = [], [], []

    def join(q):
        pair_copies[q].wait_recv()
        part[q, 1] += pair[q]

    for q in range(4):
        block_pair = pair_order[q] * 2 + (1 - core)
        block_mine = mine_order[q] * 2 + core

        for h, block in ((0, block_pair), (1, block_mine)):
            product = lax.dot_general(
                tpl[...], win[pl.ds(pl.multiple_of(block * samp, samp), samp), :],
                (((1,), (1,)), ((), ())), preferred_element_type=jnp.float32,
            )
            part[q, h] = product * factor
        copy = remote(part.at[q, 0], pair.at[q], pair_send.at[q], pair_recv.at[q], to_pair)
        copy.start()
        pair_copies.append(copy)
        if q:
            join(q - 1)
        if q in (1, 2):
            copy = remote(
                part.at[q - 1, 1], from_a.at[q - 1], a_send.at[q - 1], a_recv.at[q - 1], to_a
            )
            copy.start()
            a_copies.append(copy)
        if q == 3:
            a_copies[0].wait_recv()
            part[2, 1] += from_a[0]
            copy = remote(part.at[2, 1], from_b, b_send, b_recv, to_b)
            copy.start()
            b_copies.append(copy)
    join(3)
    a_copies[1].wait_recv()
    part[3, 1] += from_a[1]
    b_copies[0].wait_recv()
    out_ref[...] = part[3, 1] + from_b[...]
    for copy in pair_copies + a_copies + b_copies:
        copy.wait_send()

    def sent(d, carry):
        remote(
            mine.at[0], everyone.at[me], send_sem.at[d], recv_sem.at[me], target(d)
        ).wait_send()
        return carry

    lax.fori_loop(1, n, sent, 0)


def body(record, owner, offset, station, valid):
    ch_dev, samp = record.shape
    n = lax.axis_size("tm")
    parts = ch_dev // GROUP
    count = offset.shape[0]
    total = n * samp
    deep = WIN // SHIFTS * LANES
    stations = ch_dev * lax.axis_size("sta") // 3
    station = lax.all_gather(station, "sta", axis=0, tiled=True)
    valid = lax.all_gather(valid, "sta", axis=0, tiled=True)
    dma = pltpu.SemaphoreType.DMA
    f32, bf16 = jnp.float32, jnp.bfloat16
    stack = pl.pallas_call(
        functools.partial(fused_kernel, n, samp, 1.0 / math.sqrt(stations)),
        out_shape=jax.ShapeDtypeStruct((count, samp), f32),
        in_specs=[SMEM, SMEM, VMEM, VMEM, VMEM],
        out_specs=VMEM,
        scratch_shapes=[
            pltpu.VMEM((GROUP, 2 * parts, samp // 2), bf16),
            pltpu.VMEM((n, 2 * parts, samp // 2), bf16),
            pltpu.VMEM((2 * LANES, 2 * LANES), bf16),
            pltpu.VMEM((parts, total + TAIL), f32),
            pltpu.VMEM((total + LANES, LANES), f32),
            pltpu.VMEM((24 * count, LANES), f32),
            pltpu.VMEM((count, deep), bf16),
            pltpu.VMEM((GROUP * samp, LANES), f32),
            pltpu.VMEM((GROUP * samp, deep), bf16),
            pltpu.VMEM((4, 2, count, samp), f32),
            pltpu.VMEM((4, count, samp), f32),
            pltpu.VMEM((2, count, samp), f32),
            pltpu.VMEM((count, samp), f32),
            dma((n,)), dma((n,)), dma,
            dma((4,)), dma((4,)), dma((2,)), dma((2,)), dma, dma,
        ],
        compiler_params=pltpu.CompilerParams(
            collective_id=0, has_side_effects=True, vmem_limit_bytes=56 * 1024 * 1024
        ),
    )(owner.reshape(-1), offset, record, station[None, :], valid[None, :])
    stack = stack.reshape(NSTEP, TPL_STEP, samp)
    return lax.psum_scatter(stack, "sta", scatter_dimension=1, tiled=True)


def solution(mesh):
    placed = (P("sta", "tm"), P(), P(), P("sta"), P("sta"))
    return jax.shard_map(
        body, mesh=mesh, in_specs=placed, out_specs=P(None, "sta", "tm"), check_vma=False
    )
```

```python
import functools
import math

import jax
import jax.numpy as jnp
from jax import lax
from jax.experimental import pallas as pl
from jax.experimental.pallas import tpu as pltpu
from jax.sharding import PartitionSpec as P

WIN = 100
TPL_STEP = 32
NSTEP = 3
EPSILON = 1e-05
GROUP = 8
SHIFTS = 5
LANES = 128
TAIL = 256
MESH = pl.DeviceIdType.MESH
VMEM = pl.BlockSpec(memory_space=pltpu.VMEM)
SMEM = pl.BlockSpec(memory_space=pltpu.SMEM)


def ahead(array, by):
    return pltpu.roll(array, array.shape[1] - by, 1) if by else array


def window_sum(x):
    two = x + ahead(x, 1)
    four = two + ahead(two, 2)
    eight = four + ahead(four, 4)
    sixteen = eight + ahead(eight, 8)
    half = sixteen + ahead(sixteen, 16)
    full = half + ahead(half, 32)
    return full + ahead(half, 64) + ahead(four, 96)


def fused_kernel(
    n, samp, factor, owner_ref, offset_ref, record_ref, station_ref, valid_ref, out_ref,
    mine, everyone, eye, chan, rows, raw, tpl, gain, win, part, pair, from_a, from_b,
    send_sem, recv_sem, pass_send, own_sem, pair_send, pair_recv, a_send, a_recv, b_send, b_recv,
):
    me = lax.axis_index("tm")
    plane = me // GROUP
    base = plane * GROUP
    place = lax.rem(me, GROUP)
    parts = mine.shape[1] // 2
    half = samp // 2
    rows_in = SHIFTS * parts
    steps = WIN // SHIFTS
    count = owner_ref.shape[0]
    total = n * samp

    def remote(src, dst, send, recv, to):
        return pltpu.make_async_remote_copy(
            src_ref=src, dst_ref=dst, send_sem=send, recv_sem=recv,
            device_id={"tm": to}, device_id_type=MESH,
        )

    barrier = pltpu.get_barrier_semaphore()

    def greet(d, carry):
        pl.semaphore_signal(
            barrier, inc=1, device_id={"tm": lax.rem(me + d, n)}, device_id_type=MESH
        )
        return carry

    lax.fori_loop(1, n, greet, 0)
    for g in range(GROUP):
        block = record_ref[pl.ds(g * parts, parts), :]
        mine[g] = jnp.concatenate([block[:, :half], block[:, half:]], axis=0).astype(jnp.bfloat16)
    own = pltpu.make_async_copy(mine.at[place], everyone.at[me], own_sem)
    own.start()
    pl.semaphore_wait(barrier, n - 1)

    def arrived(j):
        remote(mine.at[0], everyone.at[j], send_sem.at[0], recv_sem.at[j], j).wait_recv()

    planes = n // GROUP
    below, above = plane > 0, plane < planes - 1

    def to_plane(shift, act):
        def one(d, carry):
            part_of = lax.rem(place + d, GROUP)
            act(
                remote(
                    mine.at[part_of], everyone.at[me], send_sem.at[(shift + 1) * GROUP + d],
                    recv_sem.at[me], base + shift * GROUP + part_of,
                )
            )
            return carry

        lax.fori_loop(0 if shift else 1, GROUP, one, 0)

    def all_planes(act):
        to_plane(0, act)
        pl.when(below)(lambda: to_plane(-1, act))
        pl.when(above)(lambda: to_plane(1, act))

    def handed_on(source, to):
        return remote(
            everyone.at[source], everyone.at[source], pass_send.at[source],
            recv_sem.at[source], to,
        )

    def hand_on(hops, act, wait):
        def one(d, carry):
            k = lax.rem(place + d, GROUP)

            @pl.when(plane + hops < planes)
            def from_above():
                source = base + hops * GROUP + k
                if wait:
                    arrived(source)
                pl.when(below)(lambda: act(handed_on(source, me - GROUP)))

            @pl.when(plane - hops >= 0)
            def from_below():
                source = base - hops * GROUP + k
                if wait:
                    arrived(source)
                pl.when(above)(lambda: act(handed_on(source, me + GROUP)))

            return carry

        lax.fori_loop(0, GROUP, one, 0)

    all_planes(lambda copy: copy.start())

    wide = station_ref.shape[1]
    lane = lax.broadcasted_iota(jnp.int32, (parts, wide), 1)
    row = lax.broadcasted_iota(jnp.int32, (parts, wide), 0)
    first_channel = lax.axis_index("sta") * (GROUP * parts) + place * parts
    here = lane == row + first_channel
    stations = station_ref[...].astype(jnp.float32)
    present = valid_ref[...].astype(jnp.float32)
    own_station = jnp.sum(jnp.where(here, stations, 0.0), axis=1, keepdims=True)
    own_valid = jnp.sum(jnp.where(here, present, 0.0), axis=1, keepdims=True)
    counts = jnp.sum(jnp.where(stations == own_station, present, 0.0), axis=1, keepdims=True)
    weight = own_valid / jnp.maximum(counts, 1.0)

    eye[...] = jnp.where(
        lax.broadcasted_iota(jnp.int32, eye.shape, 0) == lax.broadcasted_iota(jnp.int32, eye.shape, 1),
        1.0, 0.0,
    ).astype(jnp.bfloat16)
    chan[:, pl.ds(total, TAIL)] = jnp.zeros((parts, TAIL), jnp.float32)

    def spread(j):
        block = everyone[j].astype(jnp.float32)
        chan[:, pl.ds(pl.multiple_of(j * samp, samp), half)] = block[:parts]
        chan[:, pl.ds(pl.multiple_of(j * samp + half, half), half)] = block[parts:]

    def turn(at, length):
        values = chan[:, pl.ds(at, length + LANES)]
        pieces = [ahead(values, k)[:, :length] for k in range(SHIFTS)]
        pieces.append(jnp.zeros((LANES - rows_in, length), jnp.float32))
        wide_rows = jnp.concatenate(pieces, axis=0).astype(jnp.bfloat16)
        for cut in range(0, length, 2 * LANES):
            size = min(2 * LANES, length - cut)
            rows[pl.ds(at + cut, size), :] = lax.dot_general(
                eye[pl.ds(0, size), pl.ds(0, size)], wide_rows[:, cut : cut + size],
                (((1,), (1,)), ((), ())), preferred_element_type=jnp.float32,
            )

    own.wait()
    spread(me)

    def take_plane(d, carry):
        source = base + lax.rem(place + d, GROUP)
        arrived(source)
        spread(source)
        return carry

    lax.fori_loop(1, GROUP, take_plane, 0)
    first = pl.multiple_of(base * samp, samp)

    for i in range(GROUP - 1):
        turn(pl.multiple_of(first + i * samp, samp), samp)
    sub = 64

    def gains(at, length):
        values = chan[:, pl.ds(at, length + LANES)]
        a = window_sum(values)[:, :length] / WIN
        q = window_sum(values * values)[:, :length] / WIN
        inverse = 1.0 / jnp.sqrt(jnp.maximum(q - a * a, 0.0) + EPSILON)
        g = weight * inverse
        zeros = jnp.zeros((LANES - rows_in, length), jnp.float32)
        gain[pl.ds(pl.multiple_of(at - first, samp), length), :] = jnp.concatenate(
            [g] * SHIFTS + [zeros], axis=0
        ).T

    def gains_two(i, carry):
        gains(pl.multiple_of(first + i * (2 * samp), samp), 2 * samp)
        return carry

    def fill(r, carry):
        at = pl.multiple_of(r * sub, sub)
        scaled = gain[pl.ds(at, sub), :]
        for j in range(steps):
            x = rows[pl.ds(first + at + j * SHIFTS, sub), :]
            win[pl.ds(at, sub), pl.ds(j * LANES, LANES)] = (x * scaled).astype(jnp.bfloat16)
        return carry

    last = GROUP * samp // sub
    early = last // 2
    hand_on(1, lambda copy: copy.start(), True)
    lax.fori_loop(0, GROUP // 2 - 1, gains_two, 0)
    lax.fori_loop(0, early, fill, 0)
    for hops in range(2, planes - 1):
        hand_on(hops, lambda copy: copy.start(), True)
    after = lax.rem(base + GROUP, n)

    @pl.when(above)
    def spread_after():
        spread(after)

    turn(pl.multiple_of(first + (GROUP - 1) * samp, samp), samp)
    turn(pl.multiple_of(first + GROUP * samp, samp), LANES)
    gains_two(GROUP // 2 - 1, 0)
    lax.fori_loop(early, last, fill, 0)
    hand_on(planes - 1, lambda copy: copy.start(), True)

    def take_far(i, carry):
        e = GROUP + i * 4
        for d in range(4):
            spread(lax.rem(base + e + d, n))
        for d in range(4):
            turn(pl.multiple_of(lax.rem(base + e + d - 1, n) * samp, samp), samp)
        return carry

    lax.fori_loop(0, (n - GROUP) // 4, take_far, 0)
    turn(pl.multiple_of(lax.rem(base + n - 1, n) * samp, samp), samp)
    rows[pl.ds(total, LANES), :] = jnp.zeros((LANES, LANES), jnp.float32)

    def pick(b, carry):
        found = []
        for t in range(8):
            start = owner_ref[b * 8 + t] * samp + offset_ref[b * 8 + t]
            found.append(rows[pl.ds(start, 24, stride=SHIFTS), :])
        for t in range(8):
            raw[pl.ds(b * 8 + t, 24, stride=count), :] = found[t]
        return carry

    lax.fori_loop(0, count // 8, pick, 0)
    lane_a = lax.broadcasted_iota(jnp.int32, (LANES, LANES), 0)
    lane_b = lax.broadcasted_iota(jnp.int32, (LANES, LANES), 1)
    same = (lax.rem(lane_a, parts) == lax.rem(lane_b, parts)) & (
        (lane_a < rows_in) & (lane_b < rows_in)
    )
    fold = jnp.where(same, 1.0, 0.0).astype(jnp.float32)

    def folded(x):
        return jnp.dot(
            x, fold, precision=lax.Precision.HIGHEST, preferred_element_type=jnp.float32
        )

    sums = raw[pl.ds(0, count), :]
    for j in range(1, steps):
        sums = sums + raw[pl.ds(j * count, count), :]
    mean = folded(sums) / WIN
    square = jnp.zeros_like(mean)
    for j in range(steps):
        centred = raw[pl.ds(j * count, count), :] - mean
        square = square + centred * centred
    spread_of = jnp.sqrt(folded(square) / WIN + EPSILON)
    scale = 1.0 / (WIN * spread_of)
    for j in range(steps):
        value = (raw[pl.ds(j * count, count), :] - mean) * scale
        tpl[:, pl.ds(j * LANES, LANES)] = value.astype(jnp.bfloat16)

    core, x, y = lax.rem(place, 2), lax.rem(place // 2, 2), place // 4
    xa, ya = x + (1 - 2 * x) * (1 - core), y + (1 - 2 * y) * core
    xb, yb = x + (1 - 2 * x) * core, y + (1 - 2 * y) * (1 - core)
    own_chip, chip_a, chip_b = y * 2 + x, ya * 2 + xa, yb * 2 + xb
    diagonal = (1 - y) * 2 + (1 - x)
    mine_order = [diagonal, chip_a, chip_b, own_chip]
    pair_order = [diagonal, chip_b, chip_a, own_chip]
    to_pair = base + own_chip * 2 + (1 - core)
    to_a = base + chip_a * 2 + core
    to_b = base + chip_b * 2 + core
    pair_copies, a_copies, b_copies = [], [], []

    def join(q):
        pair_copies[q].wait_recv()
        part[q, 1] += pair[q]

    for q in range(4):
        block_pair = pair_order[q] * 2 + (1 - core)
        block_mine = mine_order[q] * 2 + core

        for h, block in ((0, block_pair), (1, block_mine)):
            product = lax.dot_general(
                tpl[...], win[pl.ds(pl.multiple_of(block * samp, samp), samp), :],
                (((1,), (1,)), ((), ())), preferred_element_type=jnp.float32,
            )
            part[q, h] = product * factor
        copy = remote(part.at[q, 0], pair.at[q], pair_send.at[q], pair_recv.at[q], to_pair)
        copy.start()
        pair_copies.append(copy)
        if q:
            join(q - 1)
        if q in (1, 2):
            copy = remote(
                part.at[q - 1, 1], from_a.at[q - 1], a_send.at[q - 1], a_recv.at[q - 1], to_a
            )
            copy.start()
            a_copies.append(copy)
        if q == 3:
            a_copies[0].wait_recv()
            part[2, 1] += from_a[0]
            copy = remote(part.at[2, 1], from_b, b_send, b_recv, to_b)
            copy.start()
            b_copies.append(copy)
    join(3)
    a_copies[1].wait_recv()
    part[3, 1] += from_a[1]
    b_copies[0].wait_recv()
    out_ref[...] = part[3, 1] + from_b[...]
    for copy in pair_copies + a_copies + b_copies:
        copy.wait_send()

    all_planes(lambda copy: copy.wait_send())
    for hops in range(1, planes):
        hand_on(hops, lambda copy: copy.wait_send(), False)


def body(record, owner, offset, station, valid):
    ch_dev, samp = record.shape
    n = lax.axis_size("tm")
    parts = ch_dev // GROUP
    count = offset.shape[0]
    total = n * samp
    deep = WIN // SHIFTS * LANES
    stations = ch_dev * lax.axis_size("sta") // 3
    station = lax.all_gather(station, "sta", axis=0, tiled=True)
    valid = lax.all_gather(valid, "sta", axis=0, tiled=True)
    dma = pltpu.SemaphoreType.DMA
    f32, bf16 = jnp.float32, jnp.bfloat16
    stack = pl.pallas_call(
        functools.partial(fused_kernel, n, samp, 1.0 / math.sqrt(stations)),
        out_shape=jax.ShapeDtypeStruct((count, samp), f32),
        in_specs=[SMEM, SMEM, VMEM, VMEM, VMEM],
        out_specs=VMEM,
        scratch_shapes=[
            pltpu.VMEM((GROUP, 2 * parts, samp // 2), bf16),
            pltpu.VMEM((n, 2 * parts, samp // 2), bf16),
            pltpu.VMEM((2 * LANES, 2 * LANES), bf16),
            pltpu.VMEM((parts, total + TAIL), f32),
            pltpu.VMEM((total + LANES, LANES), f32),
            pltpu.VMEM((24 * count, LANES), f32),
            pltpu.VMEM((count, deep), bf16),
            pltpu.VMEM((GROUP * samp, LANES), f32),
            pltpu.VMEM((GROUP * samp, deep), bf16),
            pltpu.VMEM((4, 2, count, samp), f32),
            pltpu.VMEM((4, count, samp), f32),
            pltpu.VMEM((2, count, samp), f32),
            pltpu.VMEM((count, samp), f32),
            dma((3 * GROUP,)), dma((n,)), dma((n,)), dma,
            dma((4,)), dma((4,)), dma((2,)), dma((2,)), dma, dma,
        ],
        compiler_params=pltpu.CompilerParams(
            collective_id=0, has_side_effects=True, vmem_limit_bytes=56 * 1024 * 1024
        ),
    )(owner.reshape(-1), offset, record, station[None, :], valid[None, :])
    stack = stack.reshape(NSTEP, TPL_STEP, samp)
    return lax.psum_scatter(stack, "sta", scatter_dimension=1, tiled=True)


def solution(mesh):
    placed = (P("sta", "tm"), P(), P(), P("sta"), P("sta"))
    return jax.shard_map(
        body, mesh=mesh, in_specs=placed, out_specs=P(None, "sta", "tm"), check_vma=False
    )
```

```python
import functools
import math

import jax
import jax.numpy as jnp
from jax import lax
from jax.experimental import pallas as pl
from jax.experimental.pallas import tpu as pltpu
from jax.sharding import PartitionSpec as P

WIN = 100
TPL_STEP = 32
NSTEP = 3
EPSILON = 1e-05
GROUP = 8
SHIFTS = 5
LANES = 128
TAIL = 256
MESH = pl.DeviceIdType.MESH
VMEM = pl.BlockSpec(memory_space=pltpu.VMEM)
SMEM = pl.BlockSpec(memory_space=pltpu.SMEM)


def ahead(array, by):
    return pltpu.roll(array, array.shape[1] - by, 1) if by else array


def window_sum(x):
    two = x + ahead(x, 1)
    four = two + ahead(two, 2)
    eight = four + ahead(four, 4)
    sixteen = eight + ahead(eight, 8)
    half = sixteen + ahead(sixteen, 16)
    full = half + ahead(half, 32)
    return full + ahead(half, 64) + ahead(four, 96)


def fused_kernel(
    n, samp, factor, owner_ref, offset_ref, owner_col_ref, record_ref, station_ref, valid_ref, out_ref,
    mine, everyone, eye, chan, rows, group, cut, masked, raw, tpl, gain, win, part, pair, from_a, from_b,
    send_sem, recv_sem, own_sem, pair_send, pair_recv, a_send, a_recv, b_send, b_recv,
):
    me = lax.axis_index("tm")
    plane = me // GROUP
    base = plane * GROUP
    place = lax.rem(me, GROUP)
    parts = mine.shape[1] // 2
    half = samp // 2
    rows_in = SHIFTS * parts
    steps = WIN // SHIFTS
    count = owner_ref.shape[0]
    total = n * samp

    def remote(src, dst, send, recv, to):
        return pltpu.make_async_remote_copy(
            src_ref=src, dst_ref=dst, send_sem=send, recv_sem=recv,
            device_id={"tm": to}, device_id_type=MESH,
        )

    barrier = pltpu.get_barrier_semaphore()

    def greet(d, carry):
        pl.semaphore_signal(
            barrier, inc=1, device_id={"tm": lax.rem(me + d, n)}, device_id_type=MESH
        )
        return carry

    lax.fori_loop(1, n, greet, 0)
    for g in range(GROUP):
        block = record_ref[pl.ds(g * parts, parts), :]
        mine[g] = jnp.concatenate([block[:, :half], block[:, half:]], axis=0).astype(jnp.bfloat16)
    own = pltpu.make_async_copy(mine.at[place], everyone.at[me], own_sem)
    own.start()
    pl.semaphore_wait(barrier, n - 1)

    def target(d):
        return lax.rem(base + n - (d // GROUP) * GROUP + lax.rem(place + d, GROUP), n)

    def send(d, carry):
        to = target(d)
        remote(
            mine.at[lax.rem(to, GROUP)], everyone.at[me], send_sem.at[d], recv_sem.at[me], to
        ).start()
        return carry

    lax.fori_loop(1, n, send, 0)

    wide = station_ref.shape[1]
    lane = lax.broadcasted_iota(jnp.int32, (parts, wide), 1)
    row = lax.broadcasted_iota(jnp.int32, (parts, wide), 0)
    first_channel = lax.axis_index("sta") * (GROUP * parts) + place * parts
    here = lane == row + first_channel
    stations = station_ref[...].astype(jnp.float32)
    present = valid_ref[...].astype(jnp.float32)
    own_station = jnp.sum(jnp.where(here, stations, 0.0), axis=1, keepdims=True)
    own_valid = jnp.sum(jnp.where(here, present, 0.0), axis=1, keepdims=True)
    counts = jnp.sum(jnp.where(stations == own_station, present, 0.0), axis=1, keepdims=True)
    weight = own_valid / jnp.maximum(counts, 1.0)

    eye[...] = jnp.where(
        lax.broadcasted_iota(jnp.int32, eye.shape, 0) == lax.broadcasted_iota(jnp.int32, eye.shape, 1),
        1.0, 0.0,
    ).astype(jnp.bfloat16)
    chan[:, pl.ds(total, TAIL)] = jnp.zeros((parts, TAIL), jnp.float32)

    def spread(j):
        block = everyone[j].astype(jnp.float32)
        chan[:, pl.ds(pl.multiple_of(j * samp, samp), half)] = block[:parts]
        chan[:, pl.ds(pl.multiple_of(j * samp + half, half), half)] = block[parts:]

    def arrived(j):
        remote(mine.at[0], everyone.at[j], send_sem.at[0], recv_sem.at[j], j).wait_recv()

    def transposed(pieces, dst):
        length = pieces[0].shape[1]
        blank = jnp.zeros((LANES - parts * len(pieces), length), jnp.float32)
        wide_rows = jnp.concatenate(pieces + [blank], axis=0).astype(jnp.bfloat16)
        for cut in range(0, length, 2 * LANES):
            size = min(2 * LANES, length - cut)
            dst[pl.ds(cut, size), :] = lax.dot_general(
                eye[pl.ds(0, size), pl.ds(0, size)], wide_rows[:, cut : cut + size],
                (((1,), (1,)), ((), ())), preferred_element_type=jnp.float32,
            )

    def turn(i, length):
        values = chan[:, pl.ds(pl.multiple_of(first + i * samp, samp), length + LANES)]
        transposed(
            [ahead(values, k)[:, :length] for k in range(SHIFTS)],
            rows.at[pl.ds(i * samp, length)],
        )

    def turn_group(g):
        at = [lax.rem(base + e, n) for e in range(g * SHIFTS, min(n, (g + 1) * SHIFTS))]
        transposed(
            [chan[:, pl.ds(pl.multiple_of(b * samp, samp), samp + LANES)] for b in at],
            group.at[g],
        )

    first = pl.multiple_of(base * samp, samp)
    own.wait()
    spread(me)

    def take_plane(d, carry):
        source = base + lax.rem(place + d, GROUP)
        arrived(source)
        spread(source)
        return carry

    lax.fori_loop(1, GROUP, take_plane, 0)
    for i in range(GROUP - 1):
        turn(i, samp)
    sub = 64

    def gains(at, length):
        values = chan[:, pl.ds(at, length + LANES)]
        a = window_sum(values)[:, :length] / WIN
        q = window_sum(values * values)[:, :length] / WIN
        inverse = 1.0 / jnp.sqrt(jnp.maximum(q - a * a, 0.0) + EPSILON)
        g = weight * inverse
        zeros = jnp.zeros((LANES - rows_in, length), jnp.float32)
        gain[pl.ds(pl.multiple_of(at - first, samp), length), :] = jnp.concatenate(
            [g] * SHIFTS + [zeros], axis=0
        ).T

    def gains_two(i, carry):
        gains(pl.multiple_of(first + i * (2 * samp), samp), 2 * samp)
        return carry

    def fill(r, carry):
        at = pl.multiple_of(r * sub, sub)
        scaled = gain[pl.ds(at, sub), :]
        for j in range(steps):
            x = rows[pl.ds(at + j * SHIFTS, sub), :]
            win[pl.ds(at, sub), pl.ds(j * LANES, LANES)] = (x * scaled).astype(jnp.bfloat16)
        return carry

    early = (GROUP - 2) * samp // sub
    lax.fori_loop(0, GROUP // 2 - 1, gains_two, 0)
    lax.fori_loop(0, early, fill, 0)
    after = lax.rem(base + GROUP, n)
    arrived(after)
    spread(after)
    turn(GROUP - 1, samp)
    turn(GROUP, LANES)
    gains_two(GROUP // 2 - 1, 0)
    lax.fori_loop(early, GROUP * samp // sub, fill, 0)

    taken = GROUP + 1
    for g in range(pl.cdiv(n, SHIFTS)):
        needed = min(n, (g + 1) * SHIFTS + 1)
        for e in range(taken, needed):
            source = lax.rem(base + e, n)
            arrived(source)
            spread(source)
        taken = max(taken, needed)
        turn_group(g)

    def pick(b, carry):
        for t in range(4):
            row = b * 4 + t
            after_base = lax.rem(owner_ref[row] + (n - base), n)
            g, begin = lax.div(after_base, jnp.int32(SHIFTS)), offset_ref[row]
            found = [group[g, pl.ds(begin + k, 24, stride=SHIFTS), :] for k in range(SHIFTS)]
            for k in range(SHIFTS):
                cut[k, pl.ds(row, 24, stride=count), :] = found[k]
        return carry

    lax.fori_loop(0, count // 4, pick, 0)
    held = lax.rem(lax.rem(owner_col_ref[...] + (n - base), n), jnp.int32(SHIFTS))
    lanes_of = lax.broadcasted_iota(jnp.int32, (count, LANES), 1)
    low = held * parts
    wanted = (lanes_of >= low) & (lanes_of < low + parts)
    for j in range(steps):
        for k in range(SHIFTS):
            value = jnp.where(wanted, cut[k, pl.ds(j * count, count), :], 0.0)
            masked[pl.ds(j * count, count), pl.ds(k * LANES, LANES)] = value.astype(jnp.bfloat16)
    from_lane = lax.broadcasted_iota(jnp.int32, (SHIFTS * LANES, LANES), 0)
    to_lane = lax.broadcasted_iota(jnp.int32, (SHIFTS * LANES, LANES), 1)
    moves = (
        (lax.rem(lax.rem(from_lane, LANES), parts) == lax.rem(to_lane, parts))
        & (lax.div(from_lane, LANES) == lax.div(to_lane, parts))
        & (lax.rem(from_lane, LANES) < rows_in)
    )
    raw[...] = jnp.dot(
        masked[...], jnp.where(moves, 1.0, 0.0).astype(jnp.bfloat16),
        preferred_element_type=jnp.float32,
    )
    lane_a = lax.broadcasted_iota(jnp.int32, (LANES, LANES), 0)
    lane_b = lax.broadcasted_iota(jnp.int32, (LANES, LANES), 1)
    same = (lax.rem(lane_a, parts) == lax.rem(lane_b, parts)) & (
        (lane_a < rows_in) & (lane_b < rows_in)
    )
    fold = jnp.where(same, 1.0, 0.0).astype(jnp.float32)

    def folded(x):
        return jnp.dot(
            x, fold, precision=lax.Precision.HIGHEST, preferred_element_type=jnp.float32
        )

    sums = raw[pl.ds(0, count), :]
    for j in range(1, steps):
        sums = sums + raw[pl.ds(j * count, count), :]
    mean = folded(sums) / WIN
    square = jnp.zeros_like(mean)
    for j in range(steps):
        centred = raw[pl.ds(j * count, count), :] - mean
        square = square + centred * centred
    spread_of = jnp.sqrt(folded(square) / WIN + EPSILON)
    scale = 1.0 / (WIN * spread_of)
    for j in range(steps):
        value = (raw[pl.ds(j * count, count), :] - mean) * scale
        tpl[:, pl.ds(j * LANES, LANES)] = value.astype(jnp.bfloat16)

    core, x, y = lax.rem(place, 2), lax.rem(place // 2, 2), place // 4
    xa, ya = x + (1 - 2 * x) * (1 - core), y + (1 - 2 * y) * core
    xb, yb = x + (1 - 2 * x) * core, y + (1 - 2 * y) * (1 - core)
    own_chip, chip_a, chip_b = y * 2 + x, ya * 2 + xa, yb * 2 + xb
    diagonal = (1 - y) * 2 + (1 - x)
    mine_order = [diagonal, chip_a, chip_b, own_chip]
    pair_order = [diagonal, chip_b, chip_a, own_chip]
    to_pair = base + own_chip * 2 + (1 - core)
    to_a = base + chip_a * 2 + core
    to_b = base + chip_b * 2 + core
    pair_copies, a_copies, b_copies = [], [], []

    def join(q):
        pair_copies[q].wait_recv()
        part[q, 1] += pair[q]

    for q in range(4):
        block_pair = pair_order[q] * 2 + (1 - core)
        block_mine = mine_order[q] * 2 + core

        for h, block in ((0, block_pair), (1, block_mine)):
            product = lax.dot_general(
                tpl[...], win[pl.ds(pl.multiple_of(block * samp, samp), samp), :],
                (((1,), (1,)), ((), ())), preferred_element_type=jnp.float32,
            )
            part[q, h] = product * factor
        copy = remote(part.at[q, 0], pair.at[q], pair_send.at[q], pair_recv.at[q], to_pair)
        copy.start()
        pair_copies.append(copy)
        if q:
            join(q - 1)
        if q in (1, 2):
            copy = remote(
                part.at[q - 1, 1], from_a.at[q - 1], a_send.at[q - 1], a_recv.at[q - 1], to_a
            )
            copy.start()
            a_copies.append(copy)
        if q == 3:
            a_copies[0].wait_recv()
            part[2, 1] += from_a[0]
            copy = remote(part.at[2, 1], from_b, b_send, b_recv, to_b)
            copy.start()
            b_copies.append(copy)
    join(3)
    a_copies[1].wait_recv()
    part[3, 1] += from_a[1]
    b_copies[0].wait_recv()
    out_ref[...] = part[3, 1] + from_b[...]
    for copy in pair_copies + a_copies + b_copies:
        copy.wait_send()

    def sent(d, carry):
        remote(
            mine.at[0], everyone.at[me], send_sem.at[d], recv_sem.at[me], target(d)
        ).wait_send()
        return carry

    lax.fori_loop(1, n, sent, 0)


def body(record, owner, offset, station, valid):
    ch_dev, samp = record.shape
    n = lax.axis_size("tm")
    parts = ch_dev // GROUP
    count = offset.shape[0]
    total = n * samp
    deep = WIN // SHIFTS * LANES
    stations = ch_dev * lax.axis_size("sta") // 3
    station = lax.all_gather(station, "sta", axis=0, tiled=True)
    valid = lax.all_gather(valid, "sta", axis=0, tiled=True)
    dma = pltpu.SemaphoreType.DMA
    f32, bf16 = jnp.float32, jnp.bfloat16
    stack = pl.pallas_call(
        functools.partial(fused_kernel, n, samp, 1.0 / math.sqrt(stations)),
        out_shape=jax.ShapeDtypeStruct((count, samp), f32),
        in_specs=[SMEM, SMEM, VMEM, VMEM, VMEM, VMEM],
        out_specs=VMEM,
        scratch_shapes=[
            pltpu.VMEM((GROUP, 2 * parts, samp // 2), bf16),
            pltpu.VMEM((n, 2 * parts, samp // 2), bf16),
            pltpu.VMEM((2 * LANES, 2 * LANES), bf16),
            pltpu.VMEM((parts, total + TAIL), f32),
            pltpu.VMEM((GROUP * samp + LANES, LANES), f32),
            pltpu.VMEM((pl.cdiv(n, SHIFTS), samp + LANES, LANES), f32),
            pltpu.VMEM((SHIFTS, 24 * count, LANES), f32),
            pltpu.VMEM((WIN // SHIFTS * count, SHIFTS * LANES), bf16),
            pltpu.VMEM((WIN // SHIFTS * count, LANES), f32),
            pltpu.VMEM((count, deep), bf16),
            pltpu.VMEM((GROUP * samp, LANES), f32),
            pltpu.VMEM((GROUP * samp, deep), bf16),
            pltpu.VMEM((4, 2, count, samp), f32),
            pltpu.VMEM((4, count, samp), f32),
            pltpu.VMEM((2, count, samp), f32),
            pltpu.VMEM((count, samp), f32),
            dma((n,)), dma((n,)), dma,
            dma((4,)), dma((4,)), dma((2,)), dma((2,)), dma, dma,
        ],
        compiler_params=pltpu.CompilerParams(
            collective_id=0, has_side_effects=True, vmem_limit_bytes=56 * 1024 * 1024
        ),
    )(owner.reshape(-1), offset, owner, record, station[None, :], valid[None, :])
    stack = stack.reshape(NSTEP, TPL_STEP, samp)
    return lax.psum_scatter(stack, "sta", scatter_dimension=1, tiled=True)


def solution(mesh):
    placed = (P("sta", "tm"), P(), P(), P("sta"), P("sta"))
    return jax.shard_map(
        body, mesh=mesh, in_specs=placed, out_specs=P(None, "sta", "tm"), check_vma=False
    )
```

```python
import functools
import math

import jax
import jax.numpy as jnp
from jax import lax
from jax.experimental import pallas as pl
from jax.experimental.pallas import tpu as pltpu
from jax.sharding import PartitionSpec as P

WIN = 100
TPL_STEP = 32
NSTEP = 3
EPSILON = 1e-05
GROUP = 8
SHIFTS = 5
LANES = 128
TAIL = 256
ODD = 25
MESH = pl.DeviceIdType.MESH
VMEM = pl.BlockSpec(memory_space=pltpu.VMEM)
SMEM = pl.BlockSpec(memory_space=pltpu.SMEM)


def ahead(array, by):
    return pltpu.roll(array, array.shape[1] - by, 1) if by else array


def window_sum(x):
    two = x + ahead(x, 1)
    four = two + ahead(two, 2)
    eight = four + ahead(four, 4)
    sixteen = eight + ahead(eight, 8)
    half = sixteen + ahead(sixteen, 16)
    full = half + ahead(half, 32)
    return full + ahead(half, 64) + ahead(four, 96)


def fused_kernel(
    n, samp, factor, owner_ref, offset_ref, record_ref, station_ref, valid_ref, out_ref,
    mine, everyone, eye, chan, rows, raw, tpl, gain, win, part, pair, from_a, from_b,
    send_sem, recv_sem, pass_send, own_sem, pair_send, pair_recv, a_send, a_recv, b_send, b_recv,
):
    me = lax.axis_index("tm")
    plane = me // GROUP
    base = plane * GROUP
    place = lax.rem(me, GROUP)
    parts = mine.shape[1] // 2
    half = samp // 2
    rows_in = SHIFTS * parts
    steps = WIN // SHIFTS
    count = owner_ref.shape[0]
    total = n * samp

    def remote(src, dst, send, recv, to):
        return pltpu.make_async_remote_copy(
            src_ref=src, dst_ref=dst, send_sem=send, recv_sem=recv,
            device_id={"tm": to}, device_id_type=MESH,
        )

    barrier = pltpu.get_barrier_semaphore()

    def greet(d, carry):
        pl.semaphore_signal(
            barrier, inc=1, device_id={"tm": lax.rem(me + d, n)}, device_id_type=MESH
        )
        return carry

    lax.fori_loop(1, n, greet, 0)
    for g in range(GROUP):
        block = record_ref[pl.ds(g * parts, parts), :]
        mine[g] = jnp.concatenate([block[:, :half], block[:, half:]], axis=0).astype(jnp.bfloat16)
    own = pltpu.make_async_copy(mine.at[place], everyone.at[me], own_sem)
    own.start()
    pl.semaphore_wait(barrier, n - 1)

    def arrived(j):
        remote(mine.at[0], everyone.at[j], send_sem.at[0], recv_sem.at[j], j).wait_recv()

    planes = n // GROUP
    below, above = plane > 0, plane < planes - 1

    def to_plane(shift, act):
        def one(d, carry):
            part_of = lax.rem(place + d, GROUP)
            act(
                remote(
                    mine.at[part_of], everyone.at[me], send_sem.at[(shift + 1) * GROUP + d],
                    recv_sem.at[me], base + shift * GROUP + part_of,
                )
            )
            return carry

        lax.fori_loop(0 if shift else 1, GROUP, one, 0)

    def all_planes(act):
        to_plane(0, act)
        pl.when(below)(lambda: to_plane(-1, act))
        pl.when(above)(lambda: to_plane(1, act))

    def handed_on(source, to):
        return remote(
            everyone.at[source], everyone.at[source], pass_send.at[source],
            recv_sem.at[source], to,
        )

    def hand_on(hops, act, wait):
        def one(d, carry):
            k = lax.rem(place + d, GROUP)

            @pl.when(plane + hops < planes)
            def from_above():
                source = base + hops * GROUP + k
                if wait:
                    arrived(source)
                pl.when(below)(lambda: act(handed_on(source, me - GROUP)))

            @pl.when(plane - hops >= 0)
            def from_below():
                source = base - hops * GROUP + k
                if wait:
                    arrived(source)
                pl.when(above)(lambda: act(handed_on(source, me + GROUP)))

            return carry

        lax.fori_loop(0, GROUP, one, 0)

    all_planes(lambda copy: copy.start())

    wide = station_ref.shape[1]
    lane = lax.broadcasted_iota(jnp.int32, (parts, wide), 1)
    row = lax.broadcasted_iota(jnp.int32, (parts, wide), 0)
    first_channel = lax.axis_index("sta") * (GROUP * parts) + place * parts
    here = lane == row + first_channel
    stations = station_ref[...].astype(jnp.float32)
    present = valid_ref[...].astype(jnp.float32)
    own_station = jnp.sum(jnp.where(here, stations, 0.0), axis=1, keepdims=True)
    own_valid = jnp.sum(jnp.where(here, present, 0.0), axis=1, keepdims=True)
    counts = jnp.sum(jnp.where(stations == own_station, present, 0.0), axis=1, keepdims=True)
    weight = own_valid / jnp.maximum(counts, 1.0)

    eye[...] = jnp.where(
        lax.broadcasted_iota(jnp.int32, eye.shape, 0) == lax.broadcasted_iota(jnp.int32, eye.shape, 1),
        1.0, 0.0,
    ).astype(jnp.bfloat16)
    chan[:, pl.ds(total, TAIL)] = jnp.zeros((parts, TAIL), jnp.float32)

    def spread(j):
        block = everyone[j].astype(jnp.float32)
        chan[:, pl.ds(pl.multiple_of(j * samp, samp), half)] = block[:parts]
        chan[:, pl.ds(pl.multiple_of(j * samp + half, half), half)] = block[parts:]

    def turn(at, length):
        values = chan[:, pl.ds(at, length + LANES)]
        pieces = [ahead(values, k)[:, :length] for k in range(SHIFTS)]
        pieces.append(jnp.zeros((LANES - rows_in, length), jnp.float32))
        wide_rows = jnp.concatenate(pieces, axis=0).astype(jnp.bfloat16)
        for cut in range(0, length, 2 * LANES):
            size = min(2 * LANES, length - cut)
            rows[pl.ds(at + cut, size), :] = lax.dot_general(
                eye[pl.ds(0, size), pl.ds(0, size)], wide_rows[:, cut : cut + size],
                (((1,), (1,)), ((), ())), preferred_element_type=jnp.float32,
            )

    own.wait()
    spread(me)

    def take_plane(d, carry):
        source = base + lax.rem(place + d, GROUP)
        arrived(source)
        spread(source)
        return carry

    lax.fori_loop(1, GROUP, take_plane, 0)
    first = pl.multiple_of(base * samp, samp)

    for i in range(GROUP - 1):
        turn(pl.multiple_of(first + i * samp, samp), samp)
    sub = 64

    def gains(at, length):
        values = chan[:, pl.ds(at, length + LANES)]
        a = window_sum(values)[:, :length] / WIN
        q = window_sum(values * values)[:, :length] / WIN
        inverse = 1.0 / jnp.sqrt(jnp.maximum(q - a * a, 0.0) + EPSILON)
        g = weight * inverse
        zeros = jnp.zeros((LANES - rows_in, length), jnp.float32)
        gain[pl.ds(pl.multiple_of(at - first, samp), length), :] = jnp.concatenate(
            [g] * SHIFTS + [zeros], axis=0
        ).T

    def gains_two(i, carry):
        gains(pl.multiple_of(first + i * (2 * samp), samp), 2 * samp)
        return carry

    def fill(r, carry):
        at = pl.multiple_of(r * sub, sub)
        scaled = gain[pl.ds(at, sub), :]
        for j in range(steps):
            x = rows[pl.ds(first + at + j * SHIFTS, sub), :]
            win[pl.ds(at, sub), pl.ds(j * LANES, LANES)] = (x * scaled).astype(jnp.bfloat16)
        return carry

    last = GROUP * samp // sub
    early = last // 2

    def start(copy):
        copy.start()

    def turn_block(block):
        turn(pl.multiple_of(block * samp, samp), samp)

    def take_four(block, lag, wait):
        for d in range(4):
            if wait:
                arrived(block + d)
            spread(block + d)
        for d in range(4):
            turn_block(block + d - lag)

    def take_planes(hops, wait):
        @pl.when(plane + hops < planes)
        def from_above():
            head = base + hops * GROUP

            def four(i, carry):
                take_four(head + i * 4, 1, wait)
                return carry

            lax.fori_loop(0, GROUP // 4, four, 0)
            pl.when(plane + hops == planes - 1)(lambda: turn_block(head + GROUP - 1))

        @pl.when(plane - hops >= 0)
        def from_below():
            head = base - hops * GROUP

            def four(i, carry):
                at = head + (GROUP // 4 - 1 - i) * 4
                take_four(at, 0, wait)
                return carry

            lax.fori_loop(0, GROUP // 4, four, 0)

    hand_on(1, start, True)
    lax.fori_loop(0, GROUP // 2 - 1, gains_two, 0)
    lax.fori_loop(0, early, fill, 0)
    for hops in range(2, planes - 1):
        hand_on(hops, start, True)
    pl.when(above)(lambda: spread(lax.rem(base + GROUP, n)))
    turn(pl.multiple_of(first + (GROUP - 1) * samp, samp), samp)
    turn(pl.multiple_of(first + GROUP * samp, samp), LANES)
    gains_two(GROUP // 2 - 1, 0)
    take_planes(1, False)
    lax.fori_loop(early, last, fill, 0)
    for hops in range(2, planes - 1):
        take_planes(hops, False)
    take_planes(planes - 1, True)
    rows[pl.ds(total, LANES), :] = jnp.zeros((LANES, LANES), jnp.float32)

    def pick(b, carry):
        found = []
        for t in range(8):
            begin = owner_ref[b * 8 + t] * samp + offset_ref[b * 8 + t]
            found.append(rows[pl.ds(begin, 24, stride=SHIFTS), :])
        for t in range(8):
            raw[pl.ds((b * 8 + t) * ODD, 24), :] = found[t]
        return carry

    lax.fori_loop(0, count // 8, pick, 0)

    def row_of(j):
        return raw[pl.ds(j, count, stride=ODD), :]

    lane_a = lax.broadcasted_iota(jnp.int32, (LANES, LANES), 0)
    lane_b = lax.broadcasted_iota(jnp.int32, (LANES, LANES), 1)
    same = (lax.rem(lane_a, parts) == lax.rem(lane_b, parts)) & (
        (lane_a < rows_in) & (lane_b < rows_in)
    )
    fold = jnp.where(same, 1.0, 0.0).astype(jnp.float32)

    def folded(x):
        return jnp.dot(
            x, fold, precision=lax.Precision.HIGHEST, preferred_element_type=jnp.float32
        )

    sums = row_of(0)
    for j in range(1, steps):
        sums = sums + row_of(j)
    mean = folded(sums) / WIN
    square = jnp.zeros_like(mean)
    for j in range(steps):
        centred = row_of(j) - mean
        square = square + centred * centred
    spread_of = jnp.sqrt(folded(square) / WIN + EPSILON)
    scale = 1.0 / (WIN * spread_of)
    for j in range(steps):
        value = (row_of(j) - mean) * scale
        tpl[:, pl.ds(j * LANES, LANES)] = value.astype(jnp.bfloat16)

    core, x, y = lax.rem(place, 2), lax.rem(place // 2, 2), place // 4
    xa, ya = x + (1 - 2 * x) * (1 - core), y + (1 - 2 * y) * core
    xb, yb = x + (1 - 2 * x) * core, y + (1 - 2 * y) * (1 - core)
    own_chip, chip_a, chip_b = y * 2 + x, ya * 2 + xa, yb * 2 + xb
    diagonal = (1 - y) * 2 + (1 - x)
    mine_order = [diagonal, chip_a, chip_b, own_chip]
    pair_order = [diagonal, chip_b, chip_a, own_chip]
    to_pair = base + own_chip * 2 + (1 - core)
    to_a = base + chip_a * 2 + core
    to_b = base + chip_b * 2 + core
    pair_copies, a_copies, b_copies = [], [], []

    def join(q):
        pair_copies[q].wait_recv()
        part[q, 1] += pair[q]

    for q in range(4):
        block_pair = pair_order[q] * 2 + (1 - core)
        block_mine = mine_order[q] * 2 + core

        for h, block in ((0, block_pair), (1, block_mine)):
            product = lax.dot_general(
                tpl[...], win[pl.ds(pl.multiple_of(block * samp, samp), samp), :],
                (((1,), (1,)), ((), ())), preferred_element_type=jnp.float32,
            )
            part[q, h] = product * factor
        copy = remote(part.at[q, 0], pair.at[q], pair_send.at[q], pair_recv.at[q], to_pair)
        copy.start()
        pair_copies.append(copy)
        if q:
            join(q - 1)
        if q in (1, 2):
            copy = remote(
                part.at[q - 1, 1], from_a.at[q - 1], a_send.at[q - 1], a_recv.at[q - 1], to_a
            )
            copy.start()
            a_copies.append(copy)
        if q == 3:
            a_copies[0].wait_recv()
            part[2, 1] += from_a[0]
            copy = remote(part.at[2, 1], from_b, b_send, b_recv, to_b)
            copy.start()
            b_copies.append(copy)
    join(3)
    a_copies[1].wait_recv()
    part[3, 1] += from_a[1]
    b_copies[0].wait_recv()
    out_ref[...] = part[3, 1] + from_b[...]
    for copy in pair_copies + a_copies + b_copies:
        copy.wait_send()

    all_planes(lambda copy: copy.wait_send())
    for hops in range(1, planes):
        hand_on(hops, lambda copy: copy.wait_send(), False)


def body(record, owner, offset, station, valid):
    ch_dev, samp = record.shape
    n = lax.axis_size("tm")
    parts = ch_dev // GROUP
    count = offset.shape[0]
    total = n * samp
    deep = WIN // SHIFTS * LANES
    stations = ch_dev * lax.axis_size("sta") // 3
    station = lax.all_gather(station, "sta", axis=0, tiled=True)
    valid = lax.all_gather(valid, "sta", axis=0, tiled=True)
    dma = pltpu.SemaphoreType.DMA
    f32, bf16 = jnp.float32, jnp.bfloat16
    stack = pl.pallas_call(
        functools.partial(fused_kernel, n, samp, 1.0 / math.sqrt(stations)),
        out_shape=jax.ShapeDtypeStruct((count, samp), f32),
        in_specs=[SMEM, SMEM, VMEM, VMEM, VMEM],
        out_specs=VMEM,
        scratch_shapes=[
            pltpu.VMEM((GROUP, 2 * parts, samp // 2), bf16),
            pltpu.VMEM((n, 2 * parts, samp // 2), bf16),
            pltpu.VMEM((2 * LANES, 2 * LANES), bf16),
            pltpu.VMEM((parts, total + TAIL), f32),
            pltpu.VMEM((total + LANES, LANES), f32),
            pltpu.VMEM((ODD * count, LANES), f32),
            pltpu.VMEM((count, deep), bf16),
            pltpu.VMEM((GROUP * samp, LANES), f32),
            pltpu.VMEM((GROUP * samp, deep), bf16),
            pltpu.VMEM((4, 2, count, samp), f32),
            pltpu.VMEM((4, count, samp), f32),
            pltpu.VMEM((2, count, samp), f32),
            pltpu.VMEM((count, samp), f32),
            dma((3 * GROUP,)), dma((n,)), dma((n,)), dma,
            dma((4,)), dma((4,)), dma((2,)), dma((2,)), dma, dma,
        ],
        compiler_params=pltpu.CompilerParams(
            collective_id=0, has_side_effects=True, vmem_limit_bytes=56 * 1024 * 1024
        ),
    )(owner.reshape(-1), offset, record, station[None, :], valid[None, :])
    stack = stack.reshape(NSTEP, TPL_STEP, samp)
    return lax.psum_scatter(stack, "sta", scatter_dimension=1, tiled=True)


def solution(mesh):
    placed = (P("sta", "tm"), P(), P(), P("sta"), P("sta"))
    return jax.shard_map(
        body, mesh=mesh, in_specs=placed, out_specs=P(None, "sta", "tm"), check_vma=False
    )
```

```python
import functools
import math

import jax
import jax.numpy as jnp
from jax import lax
from jax.experimental import pallas as pl
from jax.experimental.pallas import tpu as pltpu
from jax.sharding import PartitionSpec as P

WIN = 100
TPL_STEP = 32
NSTEP = 3
EPSILON = 1e-05
GROUP = 8
SHIFTS = 5
LANES = 128
TAIL = 256
ODD = 25
MESH = pl.DeviceIdType.MESH
VMEM = pl.BlockSpec(memory_space=pltpu.VMEM)
SMEM = pl.BlockSpec(memory_space=pltpu.SMEM)


def ahead(array, by):
    return pltpu.roll(array, array.shape[1] - by, 1) if by else array


def window_sum(x):
    two = x + ahead(x, 1)
    four = two + ahead(two, 2)
    eight = four + ahead(four, 4)
    sixteen = eight + ahead(eight, 8)
    half = sixteen + ahead(sixteen, 16)
    full = half + ahead(half, 32)
    return full + ahead(half, 64) + ahead(four, 96)


def fused_kernel(
    n, samp, factor, owner_ref, offset_ref, record_ref, station_ref, valid_ref, out_ref,
    mine, everyone, eye, chan, rows, raw, tpl, gain, win, part, pair, from_a, from_b,
    send_sem, recv_sem, pass_send, own_sem, pair_send, pair_recv, a_send, a_recv, b_send, b_recv,
):
    me = lax.axis_index("tm")
    plane = me // GROUP
    base = plane * GROUP
    place = lax.rem(me, GROUP)
    parts = mine.shape[1] // 2
    half = samp // 2
    rows_in = SHIFTS * parts
    steps = WIN // SHIFTS
    count = owner_ref.shape[0]
    total = n * samp

    def remote(src, dst, send, recv, to):
        return pltpu.make_async_remote_copy(
            src_ref=src, dst_ref=dst, send_sem=send, recv_sem=recv,
            device_id={"tm": to}, device_id_type=MESH,
        )

    barrier = pltpu.get_barrier_semaphore()

    def greet(d, carry):
        pl.semaphore_signal(
            barrier, inc=1, device_id={"tm": lax.rem(me + d, n)}, device_id_type=MESH
        )
        return carry

    lax.fori_loop(1, n, greet, 0)
    for g in range(GROUP):
        block = record_ref[pl.ds(g * parts, parts), :]
        mine[g] = jnp.concatenate([block[:, :half], block[:, half:]], axis=0).astype(jnp.bfloat16)
    own = pltpu.make_async_copy(mine.at[place], everyone.at[me], own_sem)
    own.start()
    pl.semaphore_wait(barrier, n - 1)

    def arrived(j):
        remote(mine.at[0], everyone.at[j], send_sem.at[0], recv_sem.at[j], j).wait_recv()

    planes = n // GROUP
    below, above = plane > 0, plane < planes - 1

    def to_plane(shift, act):
        def one(d, carry):
            part_of = lax.rem(place + d, GROUP)
            act(
                remote(
                    mine.at[part_of], everyone.at[me], send_sem.at[(shift + 1) * GROUP + d],
                    recv_sem.at[me], base + shift * GROUP + part_of,
                )
            )
            return carry

        lax.fori_loop(0 if shift else 1, GROUP, one, 0)

    def all_planes(act):
        to_plane(0, act)
        pl.when(below)(lambda: to_plane(-1, act))
        pl.when(above)(lambda: to_plane(1, act))

    def handed_on(source, to):
        return remote(
            everyone.at[source], everyone.at[source], pass_send.at[source],
            recv_sem.at[source], to,
        )

    def hand_on(hops, act, wait):
        def one(d, carry):
            k = lax.rem(place + d, GROUP)

            @pl.when(plane + hops < planes)
            def from_above():
                source = base + hops * GROUP + k
                if wait:
                    arrived(source)
                pl.when(below)(lambda: act(handed_on(source, me - GROUP)))

            @pl.when(plane - hops >= 0)
            def from_below():
                source = base - hops * GROUP + k
                if wait:
                    arrived(source)
                pl.when(above)(lambda: act(handed_on(source, me + GROUP)))

            return carry

        lax.fori_loop(0, GROUP, one, 0)

    all_planes(lambda copy: copy.start())

    wide = station_ref.shape[1]
    lane = lax.broadcasted_iota(jnp.int32, (parts, wide), 1)
    row = lax.broadcasted_iota(jnp.int32, (parts, wide), 0)
    first_channel = lax.axis_index("sta") * (GROUP * parts) + place * parts
    here = lane == row + first_channel
    stations = station_ref[...].astype(jnp.float32)
    present = valid_ref[...].astype(jnp.float32)
    own_station = jnp.sum(jnp.where(here, stations, 0.0), axis=1, keepdims=True)
    own_valid = jnp.sum(jnp.where(here, present, 0.0), axis=1, keepdims=True)
    counts = jnp.sum(jnp.where(stations == own_station, present, 0.0), axis=1, keepdims=True)
    weight = own_valid / jnp.maximum(counts, 1.0)

    eye[...] = jnp.where(
        lax.broadcasted_iota(jnp.int32, eye.shape, 0) == lax.broadcasted_iota(jnp.int32, eye.shape, 1),
        1.0, 0.0,
    ).astype(jnp.bfloat16)
    chan[:, pl.ds(total, TAIL)] = jnp.zeros((parts, TAIL), jnp.float32)

    def spread(j):
        block = everyone[j].astype(jnp.float32)
        chan[:, pl.ds(pl.multiple_of(j * samp, samp), half)] = block[:parts]
        chan[:, pl.ds(pl.multiple_of(j * samp + half, half), half)] = block[parts:]

    def turn(at, length):
        values = chan[:, pl.ds(at, length + LANES)]
        pieces = [ahead(values, k)[:, :length] for k in range(SHIFTS)]
        pieces.append(jnp.zeros((LANES - rows_in, length), jnp.float32))
        wide_rows = jnp.concatenate(pieces, axis=0).astype(jnp.bfloat16)
        for cut in range(0, length, 2 * LANES):
            size = min(2 * LANES, length - cut)
            rows[pl.ds(at + cut, size), :] = lax.dot_general(
                eye[pl.ds(0, size), pl.ds(0, size)], wide_rows[:, cut : cut + size],
                (((1,), (1,)), ((), ())), preferred_element_type=jnp.float32,
            )

    own.wait()
    spread(me)

    def take_plane(d, carry):
        source = base + lax.rem(place + d, GROUP)
        arrived(source)
        spread(source)
        return carry

    lax.fori_loop(1, GROUP, take_plane, 0)
    first = pl.multiple_of(base * samp, samp)

    for i in range(GROUP - 1):
        turn(pl.multiple_of(first + i * samp, samp), samp)
    sub = 64

    def gains(at, length):
        values = chan[:, pl.ds(at, length + LANES)]
        a = window_sum(values)[:, :length] / WIN
        q = window_sum(values * values)[:, :length] / WIN
        inverse = 1.0 / jnp.sqrt(jnp.maximum(q - a * a, 0.0) + EPSILON)
        g = weight * inverse
        zeros = jnp.zeros((LANES - rows_in, length), jnp.float32)
        gain[pl.ds(pl.multiple_of(at - first, samp), length), :] = jnp.concatenate(
            [g] * SHIFTS + [zeros], axis=0
        ).T

    def gains_two(i, carry):
        gains(pl.multiple_of(first + i * (2 * samp), samp), 2 * samp)
        return carry

    core, x, y = lax.rem(place, 2), lax.rem(place // 2, 2), place // 4
    xa, ya = x + (1 - 2 * x) * (1 - core), y + (1 - 2 * y) * core
    xb, yb = x + (1 - 2 * x) * core, y + (1 - 2 * y) * (1 - core)
    own_chip, chip_a, chip_b = y * 2 + x, ya * 2 + xa, yb * 2 + xb
    diagonal = (1 - y) * 2 + (1 - x)
    mine_order = [diagonal, chip_a, chip_b, own_chip]
    pair_order = [diagonal, chip_b, chip_a, own_chip]

    def fill(q, r):
        for h, block in ((0, pair_order[q] * 2 + (1 - core)), (1, mine_order[q] * 2 + core)):
            at = pl.multiple_of(block * samp + r * sub, sub)
            to = r * sub if isinstance(r, int) else pl.multiple_of(r * sub, sub)
            scaled = gain[pl.ds(at, sub), :]
            for j in range(steps):
                value = rows[pl.ds(first + at + j * SHIFTS, sub), :] * scaled
                win[q * 2 + h, pl.ds(to, sub), pl.ds(j * LANES, LANES)] = value.astype(jnp.bfloat16)

    def fill_pair(q):
        def one(r, carry):
            fill(q, r)
            return carry

        lax.fori_loop(0, samp // sub, one, 0)

    def start(copy):
        copy.start()

    def turn_block(block):
        turn(pl.multiple_of(block * samp, samp), samp)

    def take_four(block, lag, wait):
        for d in range(4):
            if wait:
                arrived(block + d)
            spread(block + d)
        for d in range(4):
            turn_block(block + d - lag)

    def take_planes(hops, wait):
        @pl.when(plane + hops < planes)
        def from_above():
            head = base + hops * GROUP

            def four(i, carry):
                take_four(head + i * 4, 1, wait)
                return carry

            lax.fori_loop(0, GROUP // 4, four, 0)
            pl.when(plane + hops == planes - 1)(lambda: turn_block(head + GROUP - 1))

        @pl.when(plane - hops >= 0)
        def from_below():
            head = base - hops * GROUP

            def four(i, carry):
                at = head + (GROUP // 4 - 1 - i) * 4
                take_four(at, 0, wait)
                return carry

            lax.fori_loop(0, GROUP // 4, four, 0)

    hand_on(1, start, True)
    pl.when(above)(lambda: spread(lax.rem(base + GROUP, n)))
    turn(pl.multiple_of(first + (GROUP - 1) * samp, samp), samp)
    turn(pl.multiple_of(first + GROUP * samp, samp), LANES)
    lax.fori_loop(0, GROUP // 2, gains_two, 0)
    fill_pair(0)
    for hops in range(2, planes - 1):
        hand_on(hops, start, True)
    take_planes(1, False)
    fill_pair(1)
    for hops in range(2, planes - 1):
        take_planes(hops, False)
    take_planes(planes - 1, True)
    rows[pl.ds(total, LANES), :] = jnp.zeros((LANES, LANES), jnp.float32)

    def pick(b, carry):
        found = []
        for t in range(8):
            begin = owner_ref[b * 8 + t] * samp + offset_ref[b * 8 + t]
            found.append(rows[pl.ds(begin, 24, stride=SHIFTS), :])
        for t in range(8):
            raw[pl.ds((b * 8 + t) * ODD, 24), :] = found[t]
        return carry

    lax.fori_loop(0, count // 8, pick, 0)

    def row_of(j):
        return raw[pl.ds(j, count, stride=ODD), :]

    lane_a = lax.broadcasted_iota(jnp.int32, (LANES, LANES), 0)
    lane_b = lax.broadcasted_iota(jnp.int32, (LANES, LANES), 1)
    same = (lax.rem(lane_a, parts) == lax.rem(lane_b, parts)) & (
        (lane_a < rows_in) & (lane_b < rows_in)
    )
    fold = jnp.where(same, 1.0, 0.0).astype(jnp.float32)

    def folded(x):
        return jnp.dot(
            x, fold, precision=lax.Precision.HIGHEST, preferred_element_type=jnp.float32
        )

    sums = row_of(0)
    for j in range(1, steps):
        sums = sums + row_of(j)
    mean = folded(sums) / WIN
    square = jnp.zeros_like(mean)
    for j in range(steps):
        centred = row_of(j) - mean
        square = square + centred * centred
    spread_of = jnp.sqrt(folded(square) / WIN + EPSILON)
    scale = 1.0 / (WIN * spread_of)
    for j in range(steps):
        value = (row_of(j) - mean) * scale
        tpl[:, pl.ds(j * LANES, LANES)] = value.astype(jnp.bfloat16)

    to_pair = base + own_chip * 2 + (1 - core)
    to_a = base + chip_a * 2 + core
    to_b = base + chip_b * 2 + core
    pair_copies, a_copies, b_copies = [], [], []

    def join(q):
        pair_copies[q].wait_recv()
        part[q, 1] += pair[q]

    for q in range(4):
        for h in range(2):
            product = lax.dot_general(
                tpl[...], win[q * 2 + h], (((1,), (1,)), ((), ())),
                preferred_element_type=jnp.float32,
            )
            part[q, h] = product * factor
        if q < 2:
            for r in range(samp // sub):
                fill(q + 2, r)
        copy = remote(part.at[q, 0], pair.at[q], pair_send.at[q], pair_recv.at[q], to_pair)
        copy.start()
        pair_copies.append(copy)
        if q:
            join(q - 1)
        if q in (1, 2):
            copy = remote(
                part.at[q - 1, 1], from_a.at[q - 1], a_send.at[q - 1], a_recv.at[q - 1], to_a
            )
            copy.start()
            a_copies.append(copy)
        if q == 3:
            a_copies[0].wait_recv()
            part[2, 1] += from_a[0]
            copy = remote(part.at[2, 1], from_b, b_send, b_recv, to_b)
            copy.start()
            b_copies.append(copy)
    join(3)
    a_copies[1].wait_recv()
    part[3, 1] += from_a[1]
    b_copies[0].wait_recv()
    out_ref[...] = part[3, 1] + from_b[...]
    for copy in pair_copies + a_copies + b_copies:
        copy.wait_send()

    all_planes(lambda copy: copy.wait_send())
    for hops in range(1, planes):
        hand_on(hops, lambda copy: copy.wait_send(), False)


def body(record, owner, offset, station, valid):
    ch_dev, samp = record.shape
    n = lax.axis_size("tm")
    parts = ch_dev // GROUP
    count = offset.shape[0]
    total = n * samp
    deep = WIN // SHIFTS * LANES
    stations = ch_dev * lax.axis_size("sta") // 3
    station = lax.all_gather(station, "sta", axis=0, tiled=True)
    valid = lax.all_gather(valid, "sta", axis=0, tiled=True)
    dma = pltpu.SemaphoreType.DMA
    f32, bf16 = jnp.float32, jnp.bfloat16
    stack = pl.pallas_call(
        functools.partial(fused_kernel, n, samp, 1.0 / math.sqrt(stations)),
        out_shape=jax.ShapeDtypeStruct((count, samp), f32),
        in_specs=[SMEM, SMEM, VMEM, VMEM, VMEM],
        out_specs=VMEM,
        scratch_shapes=[
            pltpu.VMEM((GROUP, 2 * parts, samp // 2), bf16),
            pltpu.VMEM((n, 2 * parts, samp // 2), bf16),
            pltpu.VMEM((2 * LANES, 2 * LANES), bf16),
            pltpu.VMEM((parts, total + TAIL), f32),
            pltpu.VMEM((total + LANES, LANES), f32),
            pltpu.VMEM((ODD * count, LANES), f32),
            pltpu.VMEM((count, deep), bf16),
            pltpu.VMEM((GROUP * samp, LANES), f32),
            pltpu.VMEM((GROUP, samp, deep), bf16),
            pltpu.VMEM((4, 2, count, samp), f32),
            pltpu.VMEM((4, count, samp), f32),
            pltpu.VMEM((2, count, samp), f32),
            pltpu.VMEM((count, samp), f32),
            dma((3 * GROUP,)), dma((n,)), dma((n,)), dma,
            dma((4,)), dma((4,)), dma((2,)), dma((2,)), dma, dma,
        ],
        compiler_params=pltpu.CompilerParams(
            collective_id=0, has_side_effects=True, vmem_limit_bytes=56 * 1024 * 1024
        ),
    )(owner.reshape(-1), offset, record, station[None, :], valid[None, :])
    stack = stack.reshape(NSTEP, TPL_STEP, samp)
    return lax.psum_scatter(stack, "sta", scatter_dimension=1, tiled=True)


def solution(mesh):
    placed = (P("sta", "tm"), P(), P(), P("sta"), P("sta"))
    return jax.shard_map(
        body, mesh=mesh, in_specs=placed, out_specs=P(None, "sta", "tm"), check_vma=False
    )
```
